32 devices in a mesh: ka: 32 (over z, y, x, core).
Axes of the slice: x: 2, y: 2, z: 4, core: 2. Of those that a mesh axis runs over, the one named last changes fastest.
Arguments:
- density: float32 [256, 128, 128], P('ka'), may hold values from 0 to 1
- hamiltonian: float32 [256, 128, 128], P('ka'), may hold values from -1 to 1
- occupations: int32 [256], P('ka'), may hold values from 56 to 72
- form_factors: bfloat16 [33, 2, 128, 128], replicated, may hold values from -0.5 to 0.5
- hartree_forms: bfloat16 [32, 128, 128], replicated, may hold values from -0.5 to 0.5
- coupling: float32 [32], replicated, may hold values from 2 to 8
Outputs:
- fock_matrix: float32 [256, 128, 128], P('ka')
- new_density: float32 [256, 128, 128], P('ka')
The draws below stay inside these ranges and needn't reach their ends.
All inputs are finite; a program needn't handle non-finite values.
Results may differ from the reference program's by a relative error of at most 0.0015.
Values may be sent and summed in bfloat16 or wider, within the bound.
No kernel may reach another device: no remote copies, remote signals or barrier semaphores. Data moves between devices by JAX's collectives and lax.ppermute only.
A program may use at most 64 MiB of HBM per device.

```python
import math
import jax
import jax.numpy as jnp
from jax import lax

NB = 128
SPAN = 16
NG = 2
NH = 32
NPUR = 6
KPTS = 256


def draw_density(key, part):
    off_key = jax.random.fold_in(key, 11)
    diag_key = jax.random.fold_in(key, 12)
    common_key = jax.random.fold_in(key, 13)
    position = jnp.arange(KPTS, dtype=jnp.float32) / (KPTS - 1)
    entries = jnp.clip(jax.random.normal(off_key, (KPTS, NB, NB), jnp.float32), -4.0, 4.0)
    own_diag = jnp.clip(jax.random.normal(diag_key, (KPTS, NB), jnp.float32), -4.0, 4.0)
    common = jnp.clip(jax.random.normal(common_key, (NB,), jnp.float32), -4.0, 4.0)
    rising = 1.0 + 2.0 * position
    weight_diag = 0.03
    spread = (entries + jnp.swapaxes(entries, 1, 2)) * (0.05 / math.sqrt(NB))
    diagonal = weight_diag * (common[None, :] + own_diag)
    identity = jnp.eye(NB, dtype=jnp.float32)
    deviation = rising[:, None, None] * (spread + diagonal[:, :, None] * identity)
    return jnp.clip(0.5 * identity + deviation, 0.0, 1.0)


def draw_hamiltonian(key, part):
    entry_key = jax.random.fold_in(key, 21)
    scale_key = jax.random.fold_in(key, 22)
    entries = jnp.clip(jax.random.normal(entry_key, (KPTS, NB, NB), jnp.float32), -4.0, 4.0)
    scales = jnp.exp(jax.random.uniform(scale_key, (KPTS, NB), jnp.float32, 0.0, math.log(3.16)))
    symmetric = (entries + jnp.swapaxes(entries, 1, 2)) * (0.3 / math.sqrt(NB))
    matrix_out = scales[:, :, None] * scales[:, None, :] * symmetric
    return jnp.clip(matrix_out, -1.0, 1.0)


def place_ends(drawn, key, low, largest):
    longest = drawn.shape.index(max(drawn.shape))
    spots = []
    for shift in (0, 1):
        where = [jax.random.randint(jax.random.fold_in(key, axis), (), 0, length) for axis, length in enumerate(drawn.shape)]
        where[longest] = (where[longest] + shift) % drawn.shape[longest]
        spots.append(tuple(where))
    return drawn.at[spots[0]].set(low).at[spots[1]].set(largest)


def noise(key, dims, scale, most, kind=jnp.bfloat16):
    return jnp.clip(scale * jax.random.normal(key, dims, jnp.float32), -most, most).astype(kind)


def setup_inputs(seed: int = 0) -> dict:
    arg_keys = jax.random.split(jax.random.key(seed), 7)
    density = draw_density(jax.random.fold_in(arg_keys[6], 71), 0)
    hamiltonian = draw_hamiltonian(jax.random.fold_in(arg_keys[6], 71), 0)
    occupations = place_ends(jax.random.randint(arg_keys[2], (KPTS,), NB // 2 - NB // 16, NB // 2 + NB // 16 + 1), jax.random.fold_in(arg_keys[2], 1), NB // 2 - NB // 16, (NB // 2 + NB // 16 + 1) - 1).astype(jnp.int32)
    form_factors = noise(arg_keys[3], (2 * SPAN + 1, NG, NB, NB), NB ** -0.5, 0.5)
    hartree_forms = noise(arg_keys[4], (NH, NB, NB), NB ** -0.5, 0.5)
    coupling = jnp.clip(jnp.exp(jax.random.uniform(arg_keys[5], (NH,), jnp.float32, math.log(2.0), math.log(8.0))), 2.0, 8.0)
    return {"density": density, "hamiltonian": hamiltonian, "occupations": occupations, "form_factors": form_factors, "hartree_forms": hartree_forms, "coupling": coupling}


def reference(density, hamiltonian, occupations, form_factors, hartree_forms, coupling):
    identity = jnp.eye(NB, dtype=jnp.float32)
    deviation = (density - 0.5 * identity).astype(jnp.bfloat16)
    forms_flat = hartree_forms.reshape(NH, NB * NB)
    partial_charge = jnp.dot(deviation.reshape(KPTS, NB * NB), forms_flat.T, preferred_element_type=jnp.float32)
    charge = lax.optimization_barrier(jnp.sum(partial_charge, axis=0)) / KPTS
    hartree = jnp.dot(coupling * charge, forms_flat.astype(jnp.float32), precision=lax.Precision.HIGHEST).reshape(NB, NB)
    wide_dev = deviation.astype(jnp.float32)
    exchange = jnp.zeros((KPTS, NB, NB), jnp.float32)
    for offset in range(2 * SPAN + 1):
        rolled = jnp.roll(wide_dev, SPAN - offset, axis=0)
        for term_index in range(NG):
            factor = form_factors[offset, term_index].astype(jnp.float32)
            half_prod = jnp.einsum('ab,kbc->kac', factor, rolled, precision=lax.Precision.HIGHEST).astype(jnp.bfloat16)
            exchange = exchange + jnp.einsum('kac,dc->kad', half_prod.astype(jnp.float32), factor, precision=lax.Precision.HIGHEST)
    combined = hamiltonian + hartree[None, :, :] - exchange
    fock_matrix = 0.5 * (combined + jnp.swapaxes(combined, 1, 2))
    traces = jnp.trace(fock_matrix, axis1=1, axis2=2)
    level_mean = jnp.sum(traces) / (KPTS * NB)
    centred = fock_matrix - level_mean * identity
    radius = jnp.sqrt(1e-06 + jnp.max(lax.optimization_barrier(jnp.sum(centred * centred, axis=(1, 2)))))
    filling = occupations.astype(jnp.float32) / NB
    purified = filling[:, None, None] * identity - 0.5 / radius * centred
    for sweep_index in range(NPUR):
        square = jnp.einsum('kab,kbc->kac', purified, purified, precision=lax.Precision.HIGHEST)
        cubed = jnp.einsum('kab,kbc->kac', square, purified, precision=lax.Precision.HIGHEST)
        purified = 3.0 * square - 2.0 * cubed
    return (fock_matrix, purified)
```

```python
import functools

import jax
import jax.numpy as jnp
from jax import lax
from jax.experimental import pallas as pl
from jax.experimental.pallas import tpu as pltpu
from jax.sharding import PartitionSpec as P

SPAN = 16
NPUR = 6
N = 128
KL = 8
CORES = 2
PACK = KL // 2 * N + 16
F32 = jnp.float32
BF16 = jnp.bfloat16
VMEM = pl.BlockSpec(memory_space=pltpu.VMEM)
SMEM = pl.BlockSpec(memory_space=pltpu.SMEM)
LANES_LAST = (((1,), (1,)), ((), ()))


def square_iota():
    row = lax.broadcasted_iota(jnp.int32, (N, N), 0)
    col = lax.broadcasted_iota(jnp.int32, (N, N), 1)
    return row, col


def params(mib):
    return pltpu.CompilerParams(vmem_limit_bytes=mib << 20)


def pack_kernel(density_ref, packed_ref, sum_ref):
    row, col = square_iota()
    half_eye = jnp.where(row == col, 0.5, 0.0).astype(F32)
    total = jnp.zeros((N, N), F32)
    diagonals = []
    for pair in range(KL // 2):
        parts = []
        for member in range(2):
            deviation = (density_ref[2 * pair + member] - half_eye).astype(BF16).astype(F32)
            total = total + deviation
            parts.append(0.5 * (deviation + deviation.T))
        packed_ref[pair * N : (pair + 1) * N, :] = jnp.where(row <= col, parts[0], parts[1]).astype(BF16)
        diagonals.append(jnp.sum(jnp.where(row == col, parts[1], 0.0), axis=0, keepdims=True))
    diagonals.append(jnp.zeros((16 - KL // 2, N), F32))
    packed_ref[KL // 2 * N :, :] = jnp.concatenate(diagonals, axis=0).astype(BF16)
    sum_ref[...] = total


def unpack(packed, blocks_ref, start):
    row, col = square_iota()
    diagonals = packed[KL // 2 * N :, :].astype(F32)
    for pair in range(KL // 2):
        both = packed[pair * N : (pair + 1) * N, :].astype(F32)
        flipped = both.T
        blocks_ref[start + 2 * pair] = jnp.where(row <= col, both, flipped).astype(BF16)
        second = jnp.where(row > col, both, jnp.where(row < col, flipped, diagonals[pair : pair + 1, :]))
        blocks_ref[start + 2 * pair + 1] = second.astype(BF16)


def both_terms(factors_ref, index):
    return jnp.concatenate([factors_ref[index, 0], factors_ref[index, 1]], axis=1)


def inner_kernel(packed_ref, factors_ref, sum_ref, forms_ref, exchange_ref, charge_ref, blocks, halves, rows):
    core = lax.rem(lax.axis_index("ka"), CORES)
    base = SPAN - (KL - 1) - KL * core
    for member in range(CORES):
        unpack(packed_ref.at[member], blocks, member * KL)

    def first(step, carry):
        right = jnp.concatenate([blocks[2 * step], blocks[2 * step + 1]], axis=1)
        left = factors_ref[pl.ds(base + 2 * step, KL + 1)].reshape((KL + 1) * 2 * N, N)
        product = jnp.dot(left, right, preferred_element_type=F32).astype(BF16)
        for shift in range(KL + 1):
            for member in range(2):
                k = member + KL - 1 - shift
                if 0 <= k < KL:
                    for term in range(2):
                        at = (shift * 2 + term) * N
                        halves[2 * step + shift, k * N : (k + 1) * N, term * N : (term + 1) * N] = product[
                            at : at + N, member * N : (member + 1) * N
                        ]
        return carry

    lax.fori_loop(0, CORES * KL // 2, first, 0)
    exchange_ref[...] = jnp.zeros_like(exchange_ref)
    for shift in range(CORES * KL + KL - 1):
        low = max(0, KL - 1 - shift)
        high = min(KL, CORES * KL + KL - 1 - shift)
        exchange_ref[low * N : high * N, :] += lax.dot_general(
            halves[shift, low * N : high * N, :],
            both_terms(factors_ref, base + shift),
            LANES_LAST,
            preferred_element_type=F32,
        )
    form_count = forms_ref.shape[0]
    for j in range(form_count):
        rows[j : j + 1, :] = jnp.sum(sum_ref[...] * forms_ref[j].astype(F32), axis=0, keepdims=True)
    charge_ref[...] = lax.dot_general(
        jnp.ones((8, N), F32), rows[...], LANES_LAST, precision=lax.Precision.HIGHEST, preferred_element_type=F32
    )


def outer_kernel(
    packed_ref, factors_ref, inner_ref, hamiltonian_ref, forms_ref, charge_ref, level_ref, stats_ref,
    blocks, near, far, exchange, traceless, rows,
):
    core = lax.rem(lax.axis_index("ka"), CORES)
    flipped = core == 1
    last = 2 * SPAN
    for member in range(CORES):
        unpack(packed_ref.at[1 - core, member], blocks, member * KL)
    unpack(packed_ref.at[core, core], blocks, CORES * KL)

    def near_factor(distance):
        return jnp.where(flipped, last - distance, distance)

    def far_factor(distance):
        return jnp.where(flipped, distance, last - distance)

    def near_block(t):
        return jnp.where(flipped, CORES * KL - 1 - t, t)

    def far_block(t):
        return CORES * KL + jnp.where(flipped, KL - 1 - t, t)

    def pair_product(first_block, second_block, shifts):
        right = jnp.concatenate([blocks[first_block], blocks[second_block]], axis=1)
        left = jnp.concatenate([factors_ref[shift].reshape(2 * N, N) for shift in shifts], axis=0)
        return jnp.dot(left, right, preferred_element_type=F32).astype(BF16)

    for step in range(CORES * KL // 2):
        distances = list(range(max(0, 2 * step - KL + 1), 2 * step + 2))
        product = pair_product(near_block(2 * step), near_block(2 * step + 1), [near_factor(d) for d in distances])
        for place, distance in enumerate(distances):
            for member in range(2):
                k = 2 * step + member - distance
                if 0 <= k < KL:
                    for term in range(2):
                        at = (place * 2 + term) * N
                        near[distance, k * N : (k + 1) * N, term * N : (term + 1) * N] = product[
                            at : at + N, member * N : (member + 1) * N
                        ]
    for step in range(KL // 2):
        distances = list(range(0, KL - 2 * step))
        product = pair_product(far_block(2 * step), far_block(2 * step + 1), [far_factor(d) for d in distances])
        for place, distance in enumerate(distances):
            for member in range(2):
                k = 2 * step + member + distance
                if 0 <= k < KL:
                    for term in range(2):
                        at = (place * 2 + term) * N
                        far[distance, k * N : (k + 1) * N, term * N : (term + 1) * N] = product[
                            at : at + N, member * N : (member + 1) * N
                        ]
    exchange[...] = jnp.zeros_like(exchange)
    for distance in range(CORES * KL):
        high = min(KL, CORES * KL - distance)
        exchange[: high * N, :] += lax.dot_general(
            near[distance, : high * N, :],
            both_terms(factors_ref, near_factor(distance)),
            LANES_LAST,
            preferred_element_type=F32,
        )
    for distance in range(KL):
        exchange[distance * N :, :] += lax.dot_general(
            far[distance, distance * N :, :],
            both_terms(factors_ref, far_factor(distance)),
            LANES_LAST,
            preferred_element_type=F32,
        )

    row, col = square_iota()
    stat_row = lax.broadcasted_iota(jnp.int32, (KL, N), 0)
    stat_col = lax.broadcasted_iota(jnp.int32, (KL, N), 1)
    stats = jnp.zeros((KL, N), F32)
    form_count = forms_ref.shape[0]
    for k in range(KL):
        mirrored = pl.multiple_of(jnp.where(flipped, KL - 1 - k, k) * N, N)
        combined = hamiltonian_ref[k] - inner_ref[k * N : (k + 1) * N, :] - exchange[pl.ds(mirrored, N), :]
        level = 0.5 * (combined + combined.T)
        level_ref[k] = level
        mean = jnp.sum(jnp.where(row == col, level, 0.0), keepdims=True) / N
        rest = level - jnp.where(row == col, mean, 0.0)
        traceless[k] = rest
        norm = jnp.sum(rest * rest, keepdims=True)
        stats = jnp.where((stat_row == k) & (stat_col == 2 * form_count), norm, stats)
        stats = jnp.where((stat_row == k) & (stat_col == 2 * form_count + 1), mean, stats)

    group = 4

    def overlaps(step, carry):
        sums = [[jnp.zeros((8, N), F32) for _ in range(group)] for _ in range(KL)]
        for part in range(N // 16):
            forms = [forms_ref[step * group + j, part * 16 : (part + 1) * 16, :].astype(F32) for j in range(group)]
            for k in range(KL):
                upper = traceless[k, part * 16 : part * 16 + 8, :]
                lower = traceless[k, part * 16 + 8 : part * 16 + 16, :]
                for j in range(group):
                    sums[k][j] = sums[k][j] + upper * forms[j][:8] + lower * forms[j][8:]
        for k in range(KL):
            for j in range(group):
                rows[k, pl.ds(step * group + j, 1), :] = jnp.sum(sums[k][j], axis=0, keepdims=True)
        return carry

    lax.fori_loop(0, form_count // group, overlaps, 0)
    pieces = jnp.zeros((KL, form_count), F32)
    short_row = lax.broadcasted_iota(jnp.int32, (KL, form_count), 0)
    for k in range(KL):
        dots = lax.dot_general(
            jnp.ones((KL, N), F32), rows[k], LANES_LAST, precision=lax.Precision.HIGHEST, preferred_element_type=F32
        )
        pieces = jnp.where(short_row == k, dots, pieces)
    charge = jnp.where(short_row == 0, charge_ref[...], 0.0)
    rest_lanes = jnp.zeros((KL, N - 2 * form_count), F32)
    stats = stats + jnp.concatenate([pieces, charge, rest_lanes], axis=1)
    stats_ref[...] = jnp.broadcast_to(stats[None], stats_ref.shape)


def final_kernel(stats_ref, level_ref, forms_ref, coupling_ref, occupations_ref, fock_ref, density_ref):
    form_count = forms_ref.shape[0]
    total = stats_ref.shape[0] * KL
    stats = stats_ref[...].reshape(total, N)
    charge = jnp.sum(stats[:, form_count : 2 * form_count], axis=0, keepdims=True) / total
    weights = coupling_ref[...] * charge
    row, col = square_iota()
    hartree = jnp.zeros((N, N), F32)
    for j in range(form_count):
        hartree = hartree + weights[:, j : j + 1] * forms_ref[j].astype(F32)
    hartree = 0.5 * (hartree + hartree.T)
    offset = jnp.sum(jnp.where(row == col, hartree, 0.0), keepdims=True) / N
    traceless = hartree - jnp.where(row == col, offset, 0.0)
    own = jnp.sum(traceless * traceless, keepdims=True)
    cross = jnp.sum(stats[:, :form_count] * weights, axis=1, keepdims=True)
    means = stats[:, 2 * form_count + 1 : 2 * form_count + 2]
    mean = jnp.sum(means, axis=0, keepdims=True) / total
    norms = stats[:, 2 * form_count : 2 * form_count + 1] + 2.0 * cross + own + N * (means - mean) ** 2
    radius = jnp.sqrt(1e-06 + jnp.max(norms, axis=0, keepdims=True))
    scale = 0.5 / radius
    shift = offset + mean
    eye = jnp.where(row == col, 1.0, 0.0).astype(F32)
    current = []
    for k in range(KL):
        fock = level_ref[k] + hartree
        fock_ref[k] = fock
        filling = occupations_ref[k].astype(F32) / N - 0.5
        current.append((filling + scale * shift) * eye - scale * fock)
    for _ in range(NPUR):
        for k in range(KL):
            short = current[k].astype(BF16)
            square = jnp.dot(short, short, preferred_element_type=F32).astype(BF16)
            cube = jnp.dot(square, short, preferred_element_type=F32)
            current[k] = 1.5 * current[k] - 2.0 * cube
    for k in range(KL):
        density_ref[k] = current[k] + 0.5 * eye


def per_device(density, hamiltonian, occupations, form_factors, hartree_forms, coupling):
    kpoint_count = density.shape[0]
    count = lax.axis_size("ka")
    form_count = hartree_forms.shape[0]
    assert kpoint_count == KL and KL * CORES == SPAN and count % CORES == 0
    shape = jax.ShapeDtypeStruct
    chips = [list(range(first, first + CORES)) for first in range(0, count, CORES)]
    packed, deviation_sum = pl.pallas_call(
        pack_kernel,
        out_shape=(shape((PACK, N), BF16), shape((N, N), F32)),
        in_specs=[VMEM],
        out_specs=(VMEM, VMEM),
        compiler_params=params(16),
    )(density)
    own_chip = lax.all_gather(packed, "ka", axis_index_groups=chips)
    pairs = [(d, (d - CORES) % count if d % CORES == 0 else (d + CORES) % count) for d in range(count)]
    neighbour = lax.ppermute(own_chip, "ka", pairs)
    inner, charge = pl.pallas_call(
        inner_kernel,
        out_shape=(shape((KL * N, N), F32), shape((8, form_count), F32)),
        in_specs=[VMEM] * 4,
        out_specs=(VMEM, VMEM),
        scratch_shapes=[
            pltpu.VMEM((CORES * KL, N, N), BF16),
            pltpu.VMEM((CORES * KL + KL - 1, KL * N, 2 * N), BF16),
            pltpu.VMEM((form_count, N), F32),
        ],
        compiler_params=params(28),
        cost_estimate=pl.CostEstimate(flops=5 * 10**9, bytes_accessed=5 * 10**6, transcendentals=0),
    )(own_chip, form_factors, deviation_sum, hartree_forms)
    outside = lax.all_gather(neighbour, "ka", axis_index_groups=chips)
    level, stats = pl.pallas_call(
        outer_kernel,
        out_shape=(shape((KL, N, N), F32), shape((count, KL, N), F32)),
        in_specs=[VMEM] * 6,
        out_specs=(VMEM, VMEM),
        scratch_shapes=[
            pltpu.VMEM((CORES * KL + KL, N, N), BF16),
            pltpu.VMEM((CORES * KL, KL * N, 2 * N), BF16),
            pltpu.VMEM((KL, KL * N, 2 * N), BF16),
            pltpu.VMEM((KL * N, N), F32),
            pltpu.VMEM((KL, N, N), F32),
            pltpu.VMEM((KL, form_count, N), F32),
        ],
        compiler_params=params(32),
    )(outside, form_factors, inner, hamiltonian, hartree_forms, charge)
    shared = lax.all_to_all(stats, "ka", 0, 0)
    return pl.pallas_call(
        final_kernel,
        out_shape=(shape((KL, N, N), F32), shape((KL, N, N), F32)),
        in_specs=[VMEM] * 4 + [SMEM],
        out_specs=(VMEM, VMEM),
        compiler_params=params(24),
    )(shared, level, hartree_forms, coupling.reshape(1, form_count), occupations)


def solution(mesh):
    placed = (P("ka", None, None), P("ka", None, None), P("ka"), P(), P(), P())
    return jax.shard_map(
        per_device,
        mesh=mesh,
        in_specs=placed,
        out_specs=(P("ka", None, None), P("ka", None, None)),
        check_vma=False,
    )
```

```python
import jax
import jax.numpy as jnp
from jax import lax
from jax.experimental import pallas as pl
from jax.experimental.pallas import tpu as pltpu
from jax.sharding import PartitionSpec as P

SPAN = 16
NPUR = 6
N = 128
KL = 8
CORES = 2
CHIP = CORES * KL
PACK = KL // 2 * N + 16
SHIFTS = CHIP + KL - 1
F32 = jnp.float32
BF16 = jnp.bfloat16
VMEM = pl.BlockSpec(memory_space=pltpu.VMEM)
SMEM = pl.BlockSpec(memory_space=pltpu.SMEM)
ANY = pl.BlockSpec(memory_space=pl.ANY)
LANES_LAST = (((1,), (1,)), ((), ()))


def square_iota():
    row = lax.broadcasted_iota(jnp.int32, (N, N), 0)
    col = lax.broadcasted_iota(jnp.int32, (N, N), 1)
    return row, col


def params(mib):
    return pltpu.CompilerParams(vmem_limit_bytes=mib << 20)


def lane_sums(rows):
    return lax.dot_general(
        jnp.ones((8, N), F32), rows, LANES_LAST, precision=lax.Precision.HIGHEST, preferred_element_type=F32
    )


def pack_kernel(density_hbm, packed_ref, sum_ref, density, arrived):
    copies = [pltpu.make_async_copy(density_hbm.at[k], density.at[k], arrived.at[k]) for k in range(KL)]
    for copy in copies:
        copy.start()
    row, col = square_iota()
    half_eye = jnp.where(row == col, 0.5, 0.0).astype(F32)
    total = jnp.zeros((N, N), F32)
    diagonals = []
    for pair in range(KL // 2):
        parts = []
        for member in range(2):
            copies[2 * pair + member].wait()
            deviation = (density[2 * pair + member] - half_eye).astype(BF16).astype(F32)
            total = total + deviation
            parts.append(0.5 * (deviation + deviation.T))
        packed_ref[pair * N : (pair + 1) * N, :] = jnp.where(row <= col, parts[0], parts[1]).astype(BF16)
        diagonals.append(jnp.sum(jnp.where(row == col, parts[1], 0.0), axis=0, keepdims=True))
    diagonals.append(jnp.zeros((16 - KL // 2, N), F32))
    packed_ref[KL // 2 * N :, :] = jnp.concatenate(diagonals, axis=0).astype(BF16)
    sum_ref[...] = total


def unpack(packed, blocks, place):
    row, col = square_iota()
    diagonals = packed[KL // 2 * N :, :].astype(F32)
    for pair in range(KL // 2):
        both = packed[pair * N : (pair + 1) * N, :].astype(F32)
        flipped = both.T
        blocks[place(2 * pair)] = jnp.where(row <= col, both, flipped).astype(BF16)
        second = jnp.where(row > col, both, jnp.where(row < col, flipped, diagonals[pair : pair + 1, :]))
        blocks[place(2 * pair + 1)] = second.astype(BF16)


def half_products(blocks, first, count, factor):
    left = blocks[first : first + count].reshape(count * N, N)
    return lax.dot_general(left, factor.reshape(2 * N, N), LANES_LAST, preferred_element_type=F32).astype(BF16)


def place_halves(products, k, slot, piece):
    lanes = slice(k % 2 * N, (k % 2 + 1) * N)
    for term in range(2):
        products[k // 2, (2 * slot + term) * N : (2 * slot + term + 1) * N, lanes] = piece[:, term * N : (term + 1) * N]


def clear_halves(products, k, slot):
    lanes = slice(k % 2 * N, (k % 2 + 1) * N)
    products[k // 2, 2 * slot * N : (2 * slot + 2) * N, lanes] = jnp.zeros((2 * N, N), BF16)


def second_product(products, pair, factors):
    left = jnp.concatenate([factor[term] for factor in factors for term in range(2)], axis=1)
    right = products[pair, : 2 * N * len(factors), :]
    return jnp.dot(left, right, preferred_element_type=F32)


def inner_kernel(
    packed_ref, factors_hbm, sum_ref, forms_hbm, exchange_ref, charge_ref,
    factors, forms, blocks, products, rows, arrived,
):
    core = lax.rem(lax.axis_index("ka"), CORES)
    base = SPAN - (KL - 1) - KL * core
    bounds = [0, 6, 12, 18, SHIFTS]
    copies = [
        pltpu.make_async_copy(
            factors_hbm.at[pl.ds(base + low, high - low)], factors.at[pl.ds(low, high - low)], arrived.at[i]
        )
        for i, (low, high) in enumerate(zip(bounds, bounds[1:]))
    ]
    forms_copy = pltpu.make_async_copy(forms_hbm, forms, arrived.at[len(copies)])
    for copy in copies + [forms_copy]:
        copy.start()
    for member in range(CORES):
        unpack(packed_ref.at[member], blocks, lambda i: member * KL + i)
    for k in range(0, KL, 2):
        clear_halves(products, k, 0)
        clear_halves(products, k + 1, CHIP)
    for shift in range(SHIFTS):
        if shift in bounds:
            copies[bounds.index(shift)].wait()
        low = max(0, KL - 1 - shift)
        high = min(KL, SHIFTS - shift)
        halves = half_products(blocks, low + shift - (KL - 1), high - low, factors[shift])
        for k in range(low, high):
            place_halves(products, k, shift - (KL - 2 - k // 2 * 2), halves[(k - low) * N : (k - low + 1) * N, :])
    for pair in range(KL // 2):
        first = KL - 2 - 2 * pair
        result = second_product(products, pair, [factors[first + slot] for slot in range(CHIP + 1)])
        for member in range(2):
            exchange_ref[2 * pair + member] = result[:, member * N : (member + 1) * N]
    forms_copy.wait()
    for j in range(forms.shape[0]):
        rows[j : j + 1, :] = jnp.sum(sum_ref[...] * forms[j].astype(F32), axis=0, keepdims=True)
    charge_ref[...] = lane_sums(rows[...])


def near_kernel(packed_ref, factors_ref, inner_ref, hamiltonian_ref, partial_ref, blocks, products):
    flipped = lax.rem(lax.axis_index("ka"), CORES) == 1
    last = 2 * SPAN
    for member in range(CORES):
        unpack(packed_ref.at[member], blocks, lambda i: jnp.where(flipped, CHIP - 1 - member * KL - i, member * KL + i))
    factors = [factors_ref.at[jnp.where(flipped, last - distance, distance)] for distance in range(CHIP)]
    for k in range(0, KL, 2):
        clear_halves(products, k + 1, CHIP - 1 - k)
    for distance in range(CHIP):
        high = min(KL, CHIP - distance)
        halves = half_products(blocks, distance, high, factors[distance][...])
        for k in range(high):
            place_halves(products, k, distance, halves[k * N : (k + 1) * N, :])
    for pair in range(KL // 2):
        result = second_product(products, pair, factors[: CHIP - 2 * pair])
        for member in range(2):
            k = 2 * pair + member
            k = jnp.where(flipped, KL - 1 - k, k)
            partial_ref[k] = hamiltonian_ref[k] - inner_ref[k] - result[:, member * N : (member + 1) * N]


def far_kernel(
    packed_ref, factors_ref, partial_ref, forms_ref, charge_ref, level_ref, stats_ref,
    blocks, products, traceless, rows,
):
    core = lax.rem(lax.axis_index("ka"), CORES)
    flipped = core == 1
    last = 2 * SPAN
    unpack(packed_ref.at[core], blocks, lambda i: jnp.where(flipped, KL - 1 - i, i))
    factors = [factors_ref.at[jnp.where(flipped, distance, last - distance)] for distance in range(KL)]
    for k in range(0, KL, 2):
        clear_halves(products, k, k + 1)
    for distance in range(KL):
        halves = half_products(blocks, 0, KL - distance, factors[distance][...])
        for k in range(distance, KL):
            place_halves(products, k, distance, halves[(k - distance) * N : (k - distance + 1) * N, :])
    row, col = square_iota()
    lane = lax.broadcasted_iota(jnp.int32, (1, N), 1)
    form_count = forms_ref.shape[0]
    numbers = jnp.zeros((1, N), F32)
    for pair in range(KL // 2):
        result = second_product(products, pair, factors[: 2 * pair + 2])
        for member in range(2):
            k = 2 * pair + member
            k = jnp.where(flipped, KL - 1 - k, k)
            combined = partial_ref[k] - result[:, member * N : (member + 1) * N]
            level = 0.5 * (combined + combined.T)
            level_ref[k] = level
            mean = jnp.sum(jnp.where(row == col, level, 0.0), keepdims=True) / N
            rest = level - jnp.where(row == col, mean, 0.0)
            traceless[k] = rest
            norm = jnp.sum(rest * rest, keepdims=True)
            numbers = jnp.where(lane == form_count + k, norm, numbers)
            numbers = jnp.where(lane == form_count + KL + k, mean, numbers)

    group = 4

    def overlaps(step, carry):
        sums = [[jnp.zeros((8, N), F32) for _ in range(group)] for _ in range(KL)]
        for part in range(N // 16):
            forms = [forms_ref[step * group + j, part * 16 : (part + 1) * 16, :].astype(F32) for j in range(group)]
            for k in range(KL):
                upper = traceless[k, part * 16 : part * 16 + 8, :]
                lower = traceless[k, part * 16 + 8 : part * 16 + 16, :]
                for j in range(group):
                    sums[k][j] = sums[k][j] + upper * forms[j][:8] + lower * forms[j][8:]
        for k in range(KL):
            for j in range(group):
                rows[pl.ds(k * form_count + step * group + j, 1), :] = jnp.sum(sums[k][j], axis=0, keepdims=True)
        return carry

    lax.fori_loop(0, form_count // group, overlaps, 0)
    charge = jnp.concatenate([charge_ref[0:1, :], jnp.zeros((1, N - form_count), F32)], axis=1)
    stats = jnp.concatenate([lane_sums(rows[...])[0:1, :], numbers + charge], axis=1)
    stats_ref[...] = jnp.broadcast_to(stats, stats_ref.shape)


def final_kernel(stats_ref, level_ref, forms_ref, coupling_ref, occupations_ref, fock_ref, density_ref):
    form_count = forms_ref.shape[0]
    count = stats_ref.shape[0]
    total = count * KL
    overlap_count = KL * form_count
    charge = jnp.sum(stats_ref[:, overlap_count : overlap_count + form_count], axis=0, keepdims=True) / total
    weights = coupling_ref[...] * charge
    row, col = square_iota()
    hartree = jnp.zeros((N, N), F32)
    for j in range(form_count):
        hartree = hartree + weights[:, j : j + 1] * forms_ref[j].astype(F32)
    hartree = 0.5 * (hartree + hartree.T)
    offset = jnp.sum(jnp.where(row == col, hartree, 0.0), keepdims=True) / N
    traceless = hartree - jnp.where(row == col, offset, 0.0)
    own = jnp.sum(traceless * traceless, keepdims=True)
    norms_at = overlap_count + form_count
    means = stats_ref[:, norms_at + KL : norms_at + 2 * KL]
    mean = jnp.sum(means, keepdims=True) / total
    cross = [
        jnp.sum(stats_ref[:, k * form_count : (k + 1) * form_count] * weights, axis=1, keepdims=True)
        for k in range(KL)
    ]
    cross = jnp.concatenate(cross, axis=1)
    norms = stats_ref[:, norms_at : norms_at + KL] + 2.0 * cross + own + N * (means - mean) ** 2
    radius = jnp.sqrt(1e-06 + jnp.max(norms, keepdims=True))
    scale = 0.5 / radius
    shift = offset + mean
    eye = jnp.where(row == col, 1.0, 0.0).astype(F32)
    current = []
    for k in range(KL):
        fock = level_ref[k] + hartree
        fock_ref[k] = fock
        filling = occupations_ref[k].astype(F32) / N - 0.5
        current.append((filling + scale * shift) * eye - scale * fock)
    for _ in range(NPUR):
        for k in range(KL):
            short = current[k].astype(BF16)
            square = jnp.dot(short, short, preferred_element_type=F32).astype(BF16)
            cube = jnp.dot(square, short, preferred_element_type=F32)
            current[k] = 1.5 * current[k] - 2.0 * cube
    for k in range(KL):
        density_ref[k] = current[k] + 0.5 * eye


def per_device(density, hamiltonian, occupations, form_factors, hartree_forms, coupling):
    kpoint_count = density.shape[0]
    count = lax.axis_size("ka")
    form_count = hartree_forms.shape[0]
    assert kpoint_count == KL and CHIP == SPAN and count % CORES == 0
    shape = jax.ShapeDtypeStruct
    chips = [list(range(first, first + CORES)) for first in range(0, count, CORES)]
    packed, deviation_sum = pl.pallas_call(
        pack_kernel,
        out_shape=(shape((PACK, N), BF16), shape((N, N), F32)),
        in_specs=[ANY],
        out_specs=(VMEM, VMEM),
        scratch_shapes=[pltpu.VMEM((KL, N, N), F32), pltpu.SemaphoreType.DMA((KL,))],
        compiler_params=params(16),
    )(density)
    own_chip = lax.all_gather(packed, "ka", axis_index_groups=chips)
    pairs = [(d, (d + CORES) % count if d % CORES == 0 else (d - CORES) % count) for d in range(count)]
    neighbour = lax.ppermute(own_chip, "ka", pairs)
    inner, charge = pl.pallas_call(
        inner_kernel,
        out_shape=(shape((KL, N, N), F32), shape((8, form_count), F32)),
        in_specs=[VMEM, ANY, VMEM, ANY],
        out_specs=(VMEM, VMEM),
        scratch_shapes=[
            pltpu.VMEM((SHIFTS, 2, N, N), BF16),
            pltpu.VMEM((form_count, N, N), BF16),
            pltpu.VMEM((CHIP, N, N), BF16),
            pltpu.VMEM((KL // 2, (CHIP + 1) * 2 * N, 2 * N), BF16),
            pltpu.VMEM((form_count, N), F32),
            pltpu.SemaphoreType.DMA((5,)),
        ],
        compiler_params=params(28),
        cost_estimate=pl.CostEstimate(flops=5 * 10**9, bytes_accessed=5 * 10**6, transcendentals=0),
    )(own_chip, form_factors, deviation_sum, hartree_forms)
    other_side = lax.ppermute(neighbour, "ka", [(d, d ^ 1) for d in range(count)])
    partial = pl.pallas_call(
        near_kernel,
        out_shape=shape((KL, N, N), F32),
        in_specs=[VMEM] * 4,
        out_specs=VMEM,
        scratch_shapes=[
            pltpu.VMEM((CHIP, N, N), BF16),
            pltpu.VMEM((KL // 2, CHIP * 2 * N, 2 * N), BF16),
        ],
        compiler_params=params(24),
        cost_estimate=pl.CostEstimate(flops=4 * 10**9, bytes_accessed=5 * 10**6, transcendentals=0),
    )(neighbour, form_factors, inner, hamiltonian)
    level, stats = pl.pallas_call(
        far_kernel,
        out_shape=(shape((KL, N, N), F32), shape((count, KL * form_count + N), F32)),
        in_specs=[VMEM] * 5,
        out_specs=(VMEM, VMEM),
        scratch_shapes=[
            pltpu.VMEM((KL, N, N), BF16),
            pltpu.VMEM((KL // 2, KL * 2 * N, 2 * N), BF16),
            pltpu.VMEM((KL, N, N), F32),
            pltpu.VMEM((KL * form_count, N), F32),
        ],
        compiler_params=params(24),
    )(other_side, form_factors, partial, hartree_forms, charge)
    shared = lax.all_to_all(stats, "ka", 0, 0, tiled=True)
    return pl.pallas_call(
        final_kernel,
        out_shape=(shape((KL, N, N), F32), shape((KL, N, N), F32)),
        in_specs=[VMEM] * 4 + [SMEM],
        out_specs=(VMEM, VMEM),
        compiler_params=params(24),
    )(shared, level, hartree_forms, coupling.reshape(1, form_count), occupations)


def solution(mesh):
    placed = (P("ka", None, None), P("ka", None, None), P("ka"), P(), P(), P())
    return jax.shard_map(
        per_device,
        mesh=mesh,
        in_specs=placed,
        out_specs=(P("ka", None, None), P("ka", None, None)),
        check_vma=False,
    )
```

```python
import functools

import jax
import jax.numpy as jnp
from jax import lax
from jax.experimental import pallas as pl
from jax.experimental.pallas import tpu as pltpu
from jax.sharding import PartitionSpec as P

SPAN = 16
NPUR = 6
N = 128
KL = 8
CORES = 2
CHIP = CORES * KL
PACK = KL // 2 * N + 16
SHIFTS = CHIP + KL - 1
F32 = jnp.float32
BF16 = jnp.bfloat16
VMEM = pl.BlockSpec(memory_space=pltpu.VMEM)
SMEM = pl.BlockSpec(memory_space=pltpu.SMEM)
HBM = pl.BlockSpec(memory_space=pltpu.HBM)
LANES_LAST = (((1,), (1,)), ((), ()))


def square_iota():
    row = lax.broadcasted_iota(jnp.int32, (N, N), 0)
    col = lax.broadcasted_iota(jnp.int32, (N, N), 1)
    return row, col


def in_hbm(array):
    return pltpu.with_memory_space_constraint(array, pltpu.HBM)


def params(mib):
    return pltpu.CompilerParams(vmem_limit_bytes=mib << 20)


def lane_sums(rows):
    return lax.dot_general(
        jnp.ones((8, N), F32), rows, LANES_LAST, precision=lax.Precision.HIGHEST, preferred_element_type=F32
    )


def pack_kernel(density_hbm, packed_ref, sum_ref, density, arrived):
    copy = pltpu.make_async_copy(density_hbm, density, arrived)
    copy.start()
    row, col = square_iota()
    half_eye = jnp.where(row == col, 0.5, 0.0).astype(F32)
    total = jnp.zeros((N, N), F32)
    diagonals = []
    copy.wait()
    for pair in range(KL // 2):
        parts = []
        for member in range(2):
            deviation = (density[2 * pair + member] - half_eye).astype(BF16).astype(F32)
            total = total + deviation
            parts.append(0.5 * (deviation + deviation.T))
        packed_ref[pair * N : (pair + 1) * N, :] = jnp.where(row <= col, parts[0], parts[1]).astype(BF16)
        diagonals.append(jnp.sum(jnp.where(row == col, parts[1], 0.0), axis=0, keepdims=True))
    diagonals.append(jnp.zeros((16 - KL // 2, N), F32))
    packed_ref[KL // 2 * N :, :] = jnp.concatenate(diagonals, axis=0).astype(BF16)
    sum_ref[...] = total


def unpack(load, blocks, place):
    row, col = square_iota()
    diagonals = load(KL // 2 * N, PACK)
    for pair in range(KL // 2):
        both = load(pair * N, (pair + 1) * N)
        flipped = both.T
        blocks[place(2 * pair)] = jnp.where(row <= col, both, flipped).astype(BF16)
        second = jnp.where(row > col, both, jnp.where(row < col, flipped, diagonals[pair : pair + 1, :]))
        blocks[place(2 * pair + 1)] = second.astype(BF16)


def own_sum_is_even():
    index = lax.axis_index("ka")
    return lax.rem(index // CORES + index, 2) == 0


def rows_of(packed_ref):
    return lambda low, high: packed_ref[low:high, :].astype(F32)


def rows_of_either(choice, first_ref, second_ref):
    return lambda low, high: jnp.where(
        choice, first_ref[low:high, :].astype(F32), second_ref[low:high, :].astype(F32)
    )


def half_products(blocks, first, count, factor):
    left = blocks[first : first + count].reshape(count * N, N)
    return lax.dot_general(left, factor.reshape(2 * N, N), LANES_LAST, preferred_element_type=F32).astype(BF16)


def place_halves(products, k, slot, piece):
    lanes = slice(k % 2 * N, (k % 2 + 1) * N)
    for term in range(2):
        products[k // 2, (2 * slot + term) * N : (2 * slot + term + 1) * N, lanes] = piece[:, term * N : (term + 1) * N]


def clear_halves(products, k, slot):
    lanes = slice(k % 2 * N, (k % 2 + 1) * N)
    products[k // 2, 2 * slot * N : (2 * slot + 2) * N, lanes] = jnp.zeros((2 * N, N), BF16)


def second_product(products, pair, factors):
    left = jnp.concatenate([factor[term] for factor in factors for term in range(2)], axis=1)
    right = products[pair, : 2 * N * len(factors), :]
    return jnp.dot(left, right, preferred_element_type=F32)


def inner_kernel(
    own_ref, other_ref, factors_ref, hamiltonian_ref, sum_ref, forms_ref, partial_ref, charge_ref,
    blocks, products, rows,
):
    core = lax.rem(lax.axis_index("ka"), CORES)
    base = SPAN - (KL - 1) - KL * core
    factors = [factors_ref.at[base + shift] for shift in range(SHIFTS)]
    unpack(rows_of(own_ref), blocks, lambda i: core * KL + i)
    unpack(rows_of(other_ref), blocks, lambda i: (1 - core) * KL + i)
    for k in range(0, KL, 2):
        clear_halves(products, k, 0)
        clear_halves(products, k + 1, CHIP)
    for shift in range(SHIFTS):
        low = max(0, KL - 1 - shift)
        high = min(KL, SHIFTS - shift)
        halves = half_products(blocks, low + shift - (KL - 1), high - low, factors[shift][...])
        for k in range(low, high):
            place_halves(products, k, shift - (KL - 2 - k // 2 * 2), halves[(k - low) * N : (k - low + 1) * N, :])
    for pair in range(KL // 2):
        first = KL - 2 - 2 * pair
        result = second_product(products, pair, factors[first : first + CHIP + 1])
        for member in range(2):
            k = 2 * pair + member
            partial_ref[k] = hamiltonian_ref[k] - result[:, member * N : (member + 1) * N]
    for j in range(forms_ref.shape[0]):
        rows[j : j + 1, :] = jnp.sum(sum_ref[...] * forms_ref[j].astype(F32), axis=0, keepdims=True)
    charge_ref[...] = lane_sums(rows[...])


def first_side_kernel(block_ref, factors_ref, partial_ref, forms_ref, next_ref, turned_ref, blocks, products, wide):
    side_kernel(False, block_ref, factors_ref, partial_ref, next_ref, blocks, products)
    form_count = forms_ref.shape[0]
    for j in range(form_count):
        wide[j * N : (j + 1) * N, :] = forms_ref[j].astype(F32)
    for row in range(N):
        turned_ref[row] = wide[pl.ds(row, form_count, stride=N), :].astype(BF16)


def side_kernel(second, block_ref, factors_ref, partial_ref, next_ref, blocks, products):
    core = lax.rem(lax.axis_index("ka"), CORES)
    far = own_sum_is_even() != second
    flipped = (core == 1) == far
    last = 2 * SPAN
    unpack(rows_of(block_ref), blocks, lambda i: jnp.where(flipped, KL - 1 - i, i))
    factors = [factors_ref.at[jnp.where(flipped, distance, last - distance)] for distance in range(KL)]
    for k in range(0, KL, 2):
        clear_halves(products, k, k + 1)
    for distance in range(KL):
        halves = half_products(blocks, 0, KL - distance, factors[distance][...])
        for k in range(distance, KL):
            place_halves(products, k, distance, halves[(k - distance) * N : (k - distance + 1) * N, :])
    for pair in range(KL // 2):
        result = second_product(products, pair, factors[: 2 * pair + 2])
        for member in range(2):
            k = 2 * pair + member
            k = jnp.where(flipped, KL - 1 - k, k)
            next_ref[k] = partial_ref[k] - result[:, member * N : (member + 1) * N]


def last_kernel(
    even_ref, odd_ref, factors_ref, partial_ref, turned_ref, charge_ref, level_ref, stats_ref,
    blocks, products, diagonals, squares,
):
    flipped = lax.rem(lax.axis_index("ka"), CORES) == 1
    last = 2 * SPAN
    unpack(rows_of_either(own_sum_is_even(), odd_ref, even_ref), blocks, lambda i: jnp.where(flipped, KL - 1 - i, i))
    factors = [factors_ref.at[jnp.where(flipped, last - distance, distance)] for distance in range(CHIP)]
    for k in range(0, KL, 2):
        clear_halves(products, k, 0)
        clear_halves(products, k + 1, KL)
    for distance in range(1, CHIP):
        low = max(0, KL - distance)
        high = min(KL, CHIP - distance)
        halves = half_products(blocks, distance + low - KL, high - low, factors[distance][...])
        for k in range(low, high):
            place_halves(products, k, distance - (KL - 1 - k // 2 * 2), halves[(k - low) * N : (k - low + 1) * N, :])
    row, col = square_iota()
    for pair in range(KL // 2):
        first = KL - 1 - 2 * pair
        result = second_product(products, pair, factors[first : first + KL + 1])
        for member in range(2):
            k = 2 * pair + member
            k = jnp.where(flipped, KL - 1 - k, k)
            combined = partial_ref[k] - result[:, member * N : (member + 1) * N]
            level = 0.5 * (combined + combined.T)
            level_ref[pl.ds(pl.multiple_of(k * N, N), N), :] = level
            diagonals[pl.ds(k, 1), :] = jnp.sum(jnp.where(row == col, level, 0.0), axis=0, keepdims=True)
            outside = jnp.where(row == col, 0.0, level)
            squares[pl.ds(k, 1), :] = jnp.sum(outside * outside, axis=0, keepdims=True)

    mean = jnp.sum(diagonals[...], axis=1, keepdims=True) / N
    rest = diagonals[...] - mean
    norm = jnp.sum(squares[...] + rest * rest, axis=1, keepdims=True)
    form_count = turned_ref.shape[1]
    lane = lax.broadcasted_iota(jnp.int32, (KL, N), 1)
    place = lax.broadcasted_iota(jnp.int32, (KL, N), 0)
    chunk = 16
    dots = jnp.zeros((2 * KL, form_count), F32)
    for start in range(0, N, chunk):
        lefts, rights = [], []
        for at in range(start, start + chunk):
            values = level_ref[pl.ds(at, KL, stride=N), :]
            values = jnp.where(lane == at, values - mean, values)
            high = values.astype(BF16).astype(F32)
            lefts.append(jnp.concatenate([high, values - high], axis=0).astype(BF16))
            rights.append(turned_ref[at])
        dots = dots + lax.dot_general(
            jnp.concatenate(lefts, axis=1), jnp.concatenate(rights, axis=1), LANES_LAST, preferred_element_type=F32
        )
    overlaps = dots[:KL, :] + dots[KL:, :]
    numbers = jnp.where(lane == form_count + place, norm, 0.0)
    numbers = numbers + jnp.where(lane == form_count + KL + place, mean, 0.0)
    charge = jnp.concatenate([charge_ref[0:1, :], jnp.zeros((1, N - form_count), F32)], axis=1)
    numbers = jnp.sum(numbers, axis=0, keepdims=True) + charge
    stats = jnp.concatenate([overlaps[k : k + 1, :] for k in range(KL)] + [numbers], axis=1)
    stats_ref[...] = jnp.broadcast_to(stats, stats_ref.shape)


def final_kernel(
    stats_ref, level_ref, forms_ref, coupling_ref, occupations_ref, fock_hbm, density_hbm, fock, density, sent
):
    form_count = forms_ref.shape[0]
    count = stats_ref.shape[0]
    total = count * KL
    overlap_count = KL * form_count
    charge = jnp.sum(stats_ref[:, overlap_count : overlap_count + form_count], axis=0, keepdims=True) / total
    weights = coupling_ref[...] * charge
    row, col = square_iota()
    hartree = jnp.zeros((N, N), F32)
    for j in range(form_count):
        hartree = hartree + weights[:, j : j + 1] * forms_ref[j].astype(F32)
    hartree = 0.5 * (hartree + hartree.T)
    offset = jnp.sum(jnp.where(row == col, hartree, 0.0), keepdims=True) / N
    traceless = hartree - jnp.where(row == col, offset, 0.0)
    own = jnp.sum(traceless * traceless, keepdims=True)
    norms_at = overlap_count + form_count
    means = stats_ref[:, norms_at + KL : norms_at + 2 * KL]
    mean = jnp.sum(means, keepdims=True) / total
    cross = [
        jnp.sum(stats_ref[:, k * form_count : (k + 1) * form_count] * weights, axis=1, keepdims=True)
        for k in range(KL)
    ]
    cross = jnp.concatenate(cross, axis=1)
    norms = stats_ref[:, norms_at : norms_at + KL] + 2.0 * cross + own + N * (means - mean) ** 2
    radius = jnp.sqrt(1e-06 + jnp.max(norms, keepdims=True))
    scale = 0.5 / radius
    shift = offset + mean
    eye = jnp.where(row == col, 1.0, 0.0).astype(F32)
    current = []
    for k in range(KL):
        fock[k] = level_ref[k * N : (k + 1) * N, :] + hartree
        filling = occupations_ref[k].astype(F32) / N - 0.5
        current.append((filling + scale * shift) * eye - scale * fock[k])
    copies = [pltpu.make_async_copy(fock, fock_hbm, sent.at[0])]
    copies[0].start()
    for _ in range(NPUR):
        for k in range(KL):
            short = current[k].astype(BF16)
            square = jnp.dot(short, short, preferred_element_type=F32).astype(BF16)
            cube = jnp.dot(square, short, preferred_element_type=F32)
            current[k] = 1.5 * current[k] - 2.0 * cube
    for k in range(KL):
        density[k] = current[k] + 0.5 * eye
        if k % 2 == 1:
            ready = pl.ds(k - 1, 2)
            copies.append(pltpu.make_async_copy(density.at[ready], density_hbm.at[ready], sent.at[(k + 1) // 2]))
            copies[-1].start()
    for copy in copies:
        copy.wait()


def per_device(density, hamiltonian, occupations, form_factors, hartree_forms, coupling):
    kpoint_count = density.shape[0]
    count = lax.axis_size("ka")
    form_count = hartree_forms.shape[0]
    assert kpoint_count == KL and CHIP == SPAN and count % CORES == 0
    shape = jax.ShapeDtypeStruct
    packed, deviation_sum = pl.pallas_call(
        pack_kernel,
        out_shape=(shape((PACK, N), BF16), shape((N, N), F32)),
        in_specs=[HBM],
        out_specs=(VMEM, VMEM),
        scratch_shapes=[pltpu.VMEM((KL, N, N), F32), pltpu.SemaphoreType.DMA(())],
        compiler_params=params(16),
        cost_estimate=pl.CostEstimate(flops=5 * 10**9, bytes_accessed=2 * 10**6, transcendentals=0),
    )(in_hbm(density))
    across = [(d, d ^ 1) for d in range(count)]
    within = [(d, d ^ CORES) for d in range(count)]
    between = [(d, ((d + CORES) ^ CORES) - CORES) for d in range(count)]
    between = [(d, target % count) for d, target in between]
    other = lax.ppermute(packed, "ka", across)
    even = lax.ppermute(packed, "ka", within)
    packed, other = lax.optimization_barrier((packed, other))
    odd = lax.ppermute(packed, "ka", between)
    partial, charge = pl.pallas_call(
        inner_kernel,
        out_shape=(shape((KL, N, N), F32), shape((8, form_count), F32)),
        in_specs=[VMEM] * 6,
        out_specs=(VMEM, VMEM),
        scratch_shapes=[
            pltpu.VMEM((CHIP, N, N), BF16),
            pltpu.VMEM((KL // 2, (CHIP + 1) * 2 * N, 2 * N), BF16),
            pltpu.VMEM((form_count, N), F32),
        ],
        compiler_params=params(28),
        cost_estimate=pl.CostEstimate(flops=5 * 10**9, bytes_accessed=5 * 10**6, transcendentals=0),
    )(packed, other, form_factors, hamiltonian, deviation_sum, hartree_forms)

    side_scratch = [pltpu.VMEM((KL, N, N), BF16), pltpu.VMEM((KL // 2, KL * 2 * N, 2 * N), BF16)]
    side_cost = pl.CostEstimate(flops=2 * 10**9, bytes_accessed=5 * 10**6, transcendentals=0)
    partial, even = lax.optimization_barrier((partial, even))
    even_across = lax.ppermute(even, "ka", across)
    partial, turned = pl.pallas_call(
        first_side_kernel,
        out_shape=(shape((KL, N, N), F32), shape((N, form_count, N), BF16)),
        in_specs=[VMEM] * 4,
        out_specs=(VMEM, VMEM),
        scratch_shapes=side_scratch + [pltpu.VMEM((form_count * N, N), F32)],
        compiler_params=params(24),
        cost_estimate=side_cost,
    )(even, form_factors, partial, hartree_forms)
    partial, odd = lax.optimization_barrier((partial, odd))
    odd_across = lax.ppermute(odd, "ka", across)
    partial = pl.pallas_call(
        functools.partial(side_kernel, True),
        out_shape=shape((KL, N, N), F32),
        in_specs=[VMEM] * 3,
        out_specs=VMEM,
        scratch_shapes=side_scratch,
        compiler_params=params(24),
        cost_estimate=side_cost,
    )(odd, form_factors, partial)
    level, stats = pl.pallas_call(
        last_kernel,
        out_shape=(shape((KL * N, N), F32), shape((count, KL * form_count + N), F32)),
        in_specs=[VMEM] * 6,
        out_specs=(VMEM, VMEM),
        scratch_shapes=[
            pltpu.VMEM((KL, N, N), BF16),
            pltpu.VMEM((KL // 2, (KL + 1) * 2 * N, 2 * N), BF16),
            pltpu.VMEM((KL, N), F32),
            pltpu.VMEM((KL, N), F32),
        ],
        compiler_params=params(28),
    )(even_across, odd_across, form_factors, partial, turned, charge)
    shared = lax.all_to_all(stats, "ka", 0, 0, tiled=True)
    return pl.pallas_call(
        final_kernel,
        out_shape=(shape((KL, N, N), F32), shape((KL, N, N), F32)),
        in_specs=[VMEM] * 4 + [SMEM],
        out_specs=(HBM, HBM),
        scratch_shapes=[pltpu.VMEM((KL, N, N), F32), pltpu.VMEM((KL, N, N), F32), pltpu.SemaphoreType.DMA((1 + KL // 2,))],
        compiler_params=params(24),
    )(shared, level, hartree_forms, coupling.reshape(1, form_count), occupations)


def solution(mesh):
    placed = (P("ka", None, None), P("ka", None, None), P("ka"), P(), P(), P())
    return jax.shard_map(
        per_device,
        mesh=mesh,
        in_specs=placed,
        out_specs=(P("ka", None, None), P("ka", None, None)),
        check_vma=False,
    )
```

```python
import functools

import jax
import jax.numpy as jnp
from jax import lax
from jax.experimental import pallas as pl
from jax.experimental.pallas import tpu as pltpu
from jax.sharding import PartitionSpec as P

SPAN = 16
NPUR = 6
N = 128
KL = 8
CORES = 2
CHIP = CORES * KL
PACK = KL // 2 * N + 16
SHIFTS = CHIP + KL - 1
F32 = jnp.float32
BF16 = jnp.bfloat16
VMEM = pl.BlockSpec(memory_space=pltpu.VMEM)
SMEM = pl.BlockSpec(memory_space=pltpu.SMEM)
HBM = pl.BlockSpec(memory_space=pltpu.HBM)
LANES_LAST = (((1,), (1,)), ((), ()))


def square_iota():
    row = lax.broadcasted_iota(jnp.int32, (N, N), 0)
    col = lax.broadcasted_iota(jnp.int32, (N, N), 1)
    return row, col


def in_hbm(array):
    return pltpu.with_memory_space_constraint(array, pltpu.HBM)


def params(mib):
    return pltpu.CompilerParams(vmem_limit_bytes=mib << 20)


def lane_sums(rows):
    return lax.dot_general(
        jnp.ones((8, N), F32), rows, LANES_LAST, precision=lax.Precision.HIGHEST, preferred_element_type=F32
    )


def pack_kernel(density_hbm, packed_ref, sum_ref, density, arrived):
    copy = pltpu.make_async_copy(density_hbm, density, arrived)
    copy.start()
    row, col = square_iota()
    half_eye = jnp.where(row == col, 0.5, 0.0).astype(F32)
    total = jnp.zeros((N, N), F32)
    diagonals = []
    copy.wait()
    for pair in range(KL // 2):
        parts = []
        for member in range(2):
            deviation = (density[2 * pair + member] - half_eye).astype(BF16).astype(F32)
            total = total + deviation
            parts.append(0.5 * (deviation + deviation.T))
        packed_ref[pair * N : (pair + 1) * N, :] = jnp.where(row <= col, parts[0], parts[1]).astype(BF16)
        diagonals.append(jnp.sum(jnp.where(row == col, parts[1], 0.0), axis=0, keepdims=True))
    diagonals.append(jnp.zeros((16 - KL // 2, N), F32))
    packed_ref[KL // 2 * N :, :] = jnp.concatenate(diagonals, axis=0).astype(BF16)
    sum_ref[...] = total


def copy_kernel(packed_ref, again_ref):
    again_ref[...] = packed_ref[...]


def unpack(load, blocks, place):
    row, col = square_iota()
    diagonals = load(KL // 2 * N, PACK)
    for pair in range(KL // 2):
        both = load(pair * N, (pair + 1) * N)
        flipped = both.T
        blocks[place(2 * pair)] = jnp.where(row <= col, both, flipped).astype(BF16)
        second = jnp.where(row > col, both, jnp.where(row < col, flipped, diagonals[pair : pair + 1, :]))
        blocks[place(2 * pair + 1)] = second.astype(BF16)


def own_sum_is_even():
    index = lax.axis_index("ka")
    return lax.rem(index // CORES + index, 2) == 0


def rows_of(packed_ref):
    return lambda low, high: packed_ref[low:high, :].astype(F32)


def rows_of_either(choice, first_ref, second_ref):
    return lambda low, high: jnp.where(
        choice, first_ref[low:high, :].astype(F32), second_ref[low:high, :].astype(F32)
    )


def half_products(blocks, first, count, factor):
    left = blocks[first : first + count].reshape(count * N, N)
    return lax.dot_general(left, factor.reshape(2 * N, N), LANES_LAST, preferred_element_type=F32).astype(BF16)


def place_halves(products, k, slot, piece):
    lanes = slice(k % 2 * N, (k % 2 + 1) * N)
    for term in range(2):
        products[k // 2, (2 * slot + term) * N : (2 * slot + term + 1) * N, lanes] = piece[:, term * N : (term + 1) * N]


def clear_halves(products, k, slot):
    lanes = slice(k % 2 * N, (k % 2 + 1) * N)
    products[k // 2, 2 * slot * N : (2 * slot + 2) * N, lanes] = jnp.zeros((2 * N, N), BF16)


def second_product(products, pair, factors):
    left = jnp.concatenate([factor[term] for factor in factors for term in range(2)], axis=1)
    right = products[pair, : 2 * N * len(factors), :]
    return jnp.dot(left, right, preferred_element_type=F32)


def inner_kernel(
    own_ref, other_ref, factors_ref, hamiltonian_ref, sum_ref, forms_ref, partial_ref, charge_ref,
    blocks, products, rows,
):
    core = lax.rem(lax.axis_index("ka"), CORES)
    base = SPAN - (KL - 1) - KL * core
    factors = [factors_ref.at[base + shift] for shift in range(SHIFTS)]
    unpack(rows_of(own_ref), blocks, lambda i: core * KL + i)
    unpack(rows_of(other_ref), blocks, lambda i: (1 - core) * KL + i)
    for k in range(0, KL, 2):
        clear_halves(products, k, 0)
        clear_halves(products, k + 1, CHIP)
    for shift in range(SHIFTS):
        low = max(0, KL - 1 - shift)
        high = min(KL, SHIFTS - shift)
        halves = half_products(blocks, low + shift - (KL - 1), high - low, factors[shift][...])
        for k in range(low, high):
            place_halves(products, k, shift - (KL - 2 - k // 2 * 2), halves[(k - low) * N : (k - low + 1) * N, :])
    for pair in range(KL // 2):
        first = KL - 2 - 2 * pair
        result = second_product(products, pair, factors[first : first + CHIP + 1])
        for member in range(2):
            k = 2 * pair + member
            partial_ref[k] = hamiltonian_ref[k] - result[:, member * N : (member + 1) * N]
    for j in range(forms_ref.shape[0]):
        rows[j : j + 1, :] = jnp.sum(sum_ref[...] * forms_ref[j].astype(F32), axis=0, keepdims=True)
    charge_ref[...] = lane_sums(rows[...])


def turn_kernel(forms_ref, turned_ref, wide):
    form_count = forms_ref.shape[0]
    for j in range(form_count):
        wide[j * N : (j + 1) * N, :] = forms_ref[j].astype(F32)
    for row in range(N):
        turned_ref[row] = wide[pl.ds(row, form_count, stride=N), :].astype(BF16)


def side_kernel(second, block_ref, factors_ref, partial_ref, next_ref, blocks, products):
    core = lax.rem(lax.axis_index("ka"), CORES)
    far = own_sum_is_even() != second
    flipped = (core == 1) == far
    last = 2 * SPAN
    unpack(rows_of(block_ref), blocks, lambda i: jnp.where(flipped, KL - 1 - i, i))
    factors = [factors_ref.at[jnp.where(flipped, distance, last - distance)] for distance in range(KL)]
    for k in range(0, KL, 2):
        clear_halves(products, k, k + 1)
    for distance in range(KL):
        halves = half_products(blocks, 0, KL - distance, factors[distance][...])
        for k in range(distance, KL):
            place_halves(products, k, distance, halves[(k - distance) * N : (k - distance + 1) * N, :])
    for pair in range(KL // 2):
        result = second_product(products, pair, factors[: 2 * pair + 2])
        for member in range(2):
            k = 2 * pair + member
            k = jnp.where(flipped, KL - 1 - k, k)
            next_ref[k] = partial_ref[k] - result[:, member * N : (member + 1) * N]


def last_kernel(
    even_ref, odd_ref, factors_ref, partial_ref, turned_ref, charge_ref, level_ref, stats_ref,
    blocks, products, diagonals, squares,
):
    flipped = lax.rem(lax.axis_index("ka"), CORES) == 1
    last = 2 * SPAN
    unpack(rows_of_either(own_sum_is_even(), odd_ref, even_ref), blocks, lambda i: jnp.where(flipped, KL - 1 - i, i))
    factors = [factors_ref.at[jnp.where(flipped, last - distance, distance)] for distance in range(CHIP)]
    for k in range(0, KL, 2):
        clear_halves(products, k, 0)
        clear_halves(products, k + 1, KL)
    for distance in range(1, CHIP):
        low = max(0, KL - distance)
        high = min(KL, CHIP - distance)
        halves = half_products(blocks, distance + low - KL, high - low, factors[distance][...])
        for k in range(low, high):
            place_halves(products, k, distance - (KL - 1 - k // 2 * 2), halves[(k - low) * N : (k - low + 1) * N, :])
    row, col = square_iota()
    for pair in range(KL // 2):
        first = KL - 1 - 2 * pair
        result = second_product(products, pair, factors[first : first + KL + 1])
        for member in range(2):
            k = 2 * pair + member
            k = jnp.where(flipped, KL - 1 - k, k)
            combined = partial_ref[k] - result[:, member * N : (member + 1) * N]
            level = 0.5 * (combined + combined.T)
            level_ref[pl.ds(pl.multiple_of(k * N, N), N), :] = level
            diagonals[pl.ds(k, 1), :] = jnp.sum(jnp.where(row == col, level, 0.0), axis=0, keepdims=True)
            outside = jnp.where(row == col, 0.0, level)
            squares[pl.ds(k, 1), :] = jnp.sum(outside * outside, axis=0, keepdims=True)

    mean = jnp.sum(diagonals[...], axis=1, keepdims=True) / N
    rest = diagonals[...] - mean
    norm = jnp.sum(squares[...] + rest * rest, axis=1, keepdims=True)
    form_count = turned_ref.shape[1]
    lane = lax.broadcasted_iota(jnp.int32, (KL, N), 1)
    place = lax.broadcasted_iota(jnp.int32, (KL, N), 0)
    chunk = 16
    dots = jnp.zeros((2 * KL, form_count), F32)
    for start in range(0, N, chunk):
        lefts, rights = [], []
        for at in range(start, start + chunk):
            values = level_ref[pl.ds(at, KL, stride=N), :]
            values = jnp.where(lane == at, values - mean, values)
            high = values.astype(BF16).astype(F32)
            lefts.append(jnp.concatenate([high, values - high], axis=0).astype(BF16))
            rights.append(turned_ref[at])
        dots = dots + lax.dot_general(
            jnp.concatenate(lefts, axis=1), jnp.concatenate(rights, axis=1), LANES_LAST, preferred_element_type=F32
        )
    overlaps = dots[:KL, :] + dots[KL:, :]
    numbers = jnp.where(lane == form_count + place, norm, 0.0)
    numbers = numbers + jnp.where(lane == form_count + KL + place, mean, 0.0)
    charge = jnp.concatenate([charge_ref[0:1, :], jnp.zeros((1, N - form_count), F32)], axis=1)
    numbers = jnp.sum(numbers, axis=0, keepdims=True) + charge
    stats = jnp.concatenate([overlaps[k : k + 1, :] for k in range(KL)] + [numbers], axis=1)
    stats_ref[...] = jnp.broadcast_to(stats, stats_ref.shape)


def final_kernel(
    stats_ref, level_ref, forms_ref, coupling_ref, occupations_ref, fock_hbm, density_hbm, fock, density, sent
):
    form_count = forms_ref.shape[0]
    count = stats_ref.shape[0]
    total = count * KL
    overlap_count = KL * form_count
    charge = jnp.sum(stats_ref[:, overlap_count : overlap_count + form_count], axis=0, keepdims=True) / total
    weights = coupling_ref[...] * charge
    row, col = square_iota()
    hartree = jnp.zeros((N, N), F32)
    for j in range(form_count):
        hartree = hartree + weights[:, j : j + 1] * forms_ref[j].astype(F32)
    hartree = 0.5 * (hartree + hartree.T)
    offset = jnp.sum(jnp.where(row == col, hartree, 0.0), keepdims=True) / N
    traceless = hartree - jnp.where(row == col, offset, 0.0)
    own = jnp.sum(traceless * traceless, keepdims=True)
    norms_at = overlap_count + form_count
    means = stats_ref[:, norms_at + KL : norms_at + 2 * KL]
    mean = jnp.sum(means, keepdims=True) / total
    cross = [
        jnp.sum(stats_ref[:, k * form_count : (k + 1) * form_count] * weights, axis=1, keepdims=True)
        for k in range(KL)
    ]
    cross = jnp.concatenate(cross, axis=1)
    norms = stats_ref[:, norms_at : norms_at + KL] + 2.0 * cross + own + N * (means - mean) ** 2
    radius = jnp.sqrt(1e-06 + jnp.max(norms, keepdims=True))
    scale = 0.5 / radius
    shift = offset + mean
    eye = jnp.where(row == col, 1.0, 0.0).astype(F32)
    current = []
    for k in range(KL):
        fock[k] = level_ref[k * N : (k + 1) * N, :] + hartree
        filling = occupations_ref[k].astype(F32) / N - 0.5
        current.append((filling + scale * shift) * eye - scale * fock[k])
    copies = [pltpu.make_async_copy(fock, fock_hbm, sent.at[0])]
    copies[0].start()
    for _ in range(NPUR):
        for k in range(KL):
            short = current[k].astype(BF16)
            square = jnp.dot(short, short, preferred_element_type=F32).astype(BF16)
            cube = jnp.dot(square, short, preferred_element_type=F32)
            current[k] = 1.5 * current[k] - 2.0 * cube
    for k in range(KL):
        density[k] = current[k] + 0.5 * eye
        if k % 2 == 1:
            ready = pl.ds(k - 1, 2)
            copies.append(pltpu.make_async_copy(density.at[ready], density_hbm.at[ready], sent.at[(k + 1) // 2]))
            copies[-1].start()
    for copy in copies:
        copy.wait()


def per_device(density, hamiltonian, occupations, form_factors, hartree_forms, coupling):
    kpoint_count = density.shape[0]
    count = lax.axis_size("ka")
    form_count = hartree_forms.shape[0]
    assert kpoint_count == KL and CHIP == SPAN and count % CORES == 0
    shape = jax.ShapeDtypeStruct
    packed, deviation_sum = pl.pallas_call(
        pack_kernel,
        out_shape=(shape((PACK, N), BF16), shape((N, N), F32)),
        in_specs=[HBM],
        out_specs=(VMEM, VMEM),
        scratch_shapes=[pltpu.VMEM((KL, N, N), F32), pltpu.SemaphoreType.DMA(())],
        compiler_params=params(16),
        cost_estimate=pl.CostEstimate(flops=5 * 10**9, bytes_accessed=2 * 10**6, transcendentals=0),
    )(in_hbm(density))
    across = [(d, d ^ 1) for d in range(count)]
    within = [(d, d ^ CORES) for d in range(count)]
    between = [(d, ((d + CORES) ^ CORES) - CORES) for d in range(count)]
    between = [(d, target % count) for d, target in between]
    other = lax.ppermute(packed, "ka", across)
    even = lax.ppermute(packed, "ka", within)
    again = pl.pallas_call(
        copy_kernel, out_shape=shape((PACK, N), BF16), in_specs=[VMEM], out_specs=VMEM, compiler_params=params(16)
    )(packed)
    odd = lax.ppermute(again, "ka", between)
    partial, charge = pl.pallas_call(
        inner_kernel,
        out_shape=(shape((KL, N, N), F32), shape((8, form_count), F32)),
        in_specs=[VMEM] * 6,
        out_specs=(VMEM, VMEM),
        scratch_shapes=[
            pltpu.VMEM((CHIP, N, N), BF16),
            pltpu.VMEM((KL // 2, (CHIP + 1) * 2 * N, 2 * N), BF16),
            pltpu.VMEM((form_count, N), F32),
        ],
        compiler_params=params(28),
        cost_estimate=pl.CostEstimate(flops=5 * 10**9, bytes_accessed=5 * 10**6, transcendentals=0),
    )(packed, other, form_factors, hamiltonian, deviation_sum, hartree_forms)

    side_cost = pl.CostEstimate(flops=2 * 10**9, bytes_accessed=5 * 10**6, transcendentals=0)

    def side(second, block, partial):
        return pl.pallas_call(
            functools.partial(side_kernel, second),
            out_shape=shape((KL, N, N), F32),
            in_specs=[VMEM] * 3,
            out_specs=VMEM,
            scratch_shapes=[pltpu.VMEM((KL, N, N), BF16), pltpu.VMEM((KL // 2, KL * 2 * N, 2 * N), BF16)],
            compiler_params=params(24),
            cost_estimate=side_cost,
        )(block, form_factors, partial)

    partial, hartree_forms = lax.optimization_barrier((partial, hartree_forms))
    turned = pl.pallas_call(
        turn_kernel,
        out_shape=shape((N, form_count, N), BF16),
        in_specs=[VMEM],
        out_specs=VMEM,
        scratch_shapes=[pltpu.VMEM((form_count * N, N), F32)],
        compiler_params=params(16),
        cost_estimate=side_cost,
    )(hartree_forms)
    partial, turned, even = lax.optimization_barrier((partial, turned, even))
    even_across = lax.ppermute(even, "ka", across)
    partial = side(False, even, partial)
    partial, odd = lax.optimization_barrier((partial, odd))
    odd_across = lax.ppermute(odd, "ka", across)
    partial = side(True, odd, partial)
    level, stats = pl.pallas_call(
        last_kernel,
        out_shape=(shape((KL * N, N), F32), shape((count, KL * form_count + N), F32)),
        in_specs=[VMEM] * 6,
        out_specs=(VMEM, VMEM),
        scratch_shapes=[
            pltpu.VMEM((KL, N, N), BF16),
            pltpu.VMEM((KL // 2, (KL + 1) * 2 * N, 2 * N), BF16),
            pltpu.VMEM((KL, N), F32),
            pltpu.VMEM((KL, N), F32),
        ],
        compiler_params=params(28),
    )(even_across, odd_across, form_factors, partial, turned, charge)
    shared = lax.all_to_all(stats, "ka", 0, 0, tiled=True)
    return pl.pallas_call(
        final_kernel,
        out_shape=(shape((KL, N, N), F32), shape((KL, N, N), F32)),
        in_specs=[VMEM] * 4 + [SMEM],
        out_specs=(HBM, HBM),
        scratch_shapes=[pltpu.VMEM((KL, N, N), F32), pltpu.VMEM((KL, N, N), F32), pltpu.SemaphoreType.DMA((1 + KL // 2,))],
        compiler_params=params(24),
    )(shared, level, hartree_forms, coupling.reshape(1, form_count), occupations)


def solution(mesh):
    placed = (P("ka", None, None), P("ka", None, None), P("ka"), P(), P(), P())
    return jax.shard_map(
        per_device,
        mesh=mesh,
        in_specs=placed,
        out_specs=(P("ka", None, None), P("ka", None, None)),
        check_vma=False,
    )
```

```python
import functools

import jax
import jax.numpy as jnp
from jax import lax
from jax.experimental import pallas as pl
from jax.experimental.pallas import tpu as pltpu
from jax.sharding import PartitionSpec as P

SPAN = 16
NPUR = 6
N = 128
KL = 8
CORES = 2
CHIP = CORES * KL
PACK = KL // 2 * N + 16
SHIFTS = CHIP + KL - 1
F32 = jnp.float32
BF16 = jnp.bfloat16
VMEM = pl.BlockSpec(memory_space=pltpu.VMEM)
SMEM = pl.BlockSpec(memory_space=pltpu.SMEM)
HBM = pl.BlockSpec(memory_space=pltpu.HBM)
LANES_LAST = (((1,), (1,)), ((), ()))


def square_iota():
    row = lax.broadcasted_iota(jnp.int32, (N, N), 0)
    col = lax.broadcasted_iota(jnp.int32, (N, N), 1)
    return row, col


def in_hbm(array):
    return pltpu.with_memory_space_constraint(array, pltpu.HBM)


def params(mib):
    return pltpu.CompilerParams(vmem_limit_bytes=mib << 20)


def lane_sums(rows):
    return lax.dot_general(
        jnp.ones((8, N), F32), rows, LANES_LAST, precision=lax.Precision.HIGHEST, preferred_element_type=F32
    )


def pack_kernel(density_hbm, packed_ref, sum_ref, density, arrived):
    copy = pltpu.make_async_copy(density_hbm, density, arrived)
    copy.start()
    row, col = square_iota()
    half_eye = jnp.where(row == col, 0.5, 0.0).astype(F32)
    total = jnp.zeros((N, N), F32)
    diagonals = []
    copy.wait()
    for pair in range(KL // 2):
        parts = []
        for member in range(2):
            deviation = (density[2 * pair + member] - half_eye).astype(BF16).astype(F32)
            total = total + deviation
            parts.append(0.5 * (deviation + deviation.T))
        packed_ref[pair * N : (pair + 1) * N, :] = jnp.where(row <= col, parts[0], parts[1]).astype(BF16)
        diagonals.append(jnp.sum(jnp.where(row == col, parts[1], 0.0), axis=0, keepdims=True))
    diagonals.append(jnp.zeros((16 - KL // 2, N), F32))
    packed_ref[KL // 2 * N :, :] = jnp.concatenate(diagonals, axis=0).astype(BF16)
    sum_ref[...] = total


def copy_kernel(packed_ref, again_ref):
    again_ref[...] = packed_ref[...]


def unpack(load, blocks, place):
    row, col = square_iota()
    diagonals = load(KL // 2 * N, PACK)
    for pair in range(KL // 2):
        both = load(pair * N, (pair + 1) * N)
        flipped = both.T
        blocks[place(2 * pair)] = jnp.where(row <= col, both, flipped).astype(BF16)
        second = jnp.where(row > col, both, jnp.where(row < col, flipped, diagonals[pair : pair + 1, :]))
        blocks[place(2 * pair + 1)] = second.astype(BF16)


def own_sum_is_even():
    index = lax.axis_index("ka")
    return lax.rem(index // CORES + index, 2) == 0


def rows_of(packed_ref):
    return lambda low, high: packed_ref[low:high, :].astype(F32)


def rows_of_either(choice, first_ref, second_ref):
    return lambda low, high: jnp.where(
        choice, first_ref[low:high, :].astype(F32), second_ref[low:high, :].astype(F32)
    )


def half_products(blocks, first, count, factor):
    left = blocks[first : first + count].reshape(count * N, N)
    return lax.dot_general(left, factor.reshape(2 * N, N), LANES_LAST, preferred_element_type=F32).astype(BF16)


def place_halves(products, k, slot, piece):
    lanes = slice(k % 2 * N, (k % 2 + 1) * N)
    for term in range(2):
        products[k // 2, (2 * slot + term) * N : (2 * slot + term + 1) * N, lanes] = piece[:, term * N : (term + 1) * N]


def clear_halves(products, k, slot):
    lanes = slice(k % 2 * N, (k % 2 + 1) * N)
    products[k // 2, 2 * slot * N : (2 * slot + 2) * N, lanes] = jnp.zeros((2 * N, N), BF16)


def second_product(products, pair, factors):
    left = jnp.concatenate([factor[term] for factor in factors for term in range(2)], axis=1)
    right = products[pair, : 2 * N * len(factors), :]
    return jnp.dot(left, right, preferred_element_type=F32)


def inner_kernel(
    own_ref, other_ref, factors_ref, hamiltonian_ref, sum_ref, forms_ref, partial_ref, charge_ref,
    blocks, products, rows,
):
    core = lax.rem(lax.axis_index("ka"), CORES)
    base = SPAN - (KL - 1) - KL * core
    factors = [factors_ref.at[base + shift] for shift in range(SHIFTS)]
    unpack(rows_of(own_ref), blocks, lambda i: core * KL + i)
    unpack(rows_of(other_ref), blocks, lambda i: (1 - core) * KL + i)
    for k in range(0, KL, 2):
        clear_halves(products, k, 0)
        clear_halves(products, k + 1, CHIP)
    for shift in range(SHIFTS):
        low = max(0, KL - 1 - shift)
        high = min(KL, SHIFTS - shift)
        halves = half_products(blocks, low + shift - (KL - 1), high - low, factors[shift][...])
        for k in range(low, high):
            place_halves(products, k, shift - (KL - 2 - k // 2 * 2), halves[(k - low) * N : (k - low + 1) * N, :])
    for pair in range(KL // 2):
        first = KL - 2 - 2 * pair
        result = second_product(products, pair, factors[first : first + CHIP + 1])
        for member in range(2):
            k = 2 * pair + member
            partial_ref[k] = hamiltonian_ref[k] - result[:, member * N : (member + 1) * N]
    for j in range(forms_ref.shape[0]):
        rows[j : j + 1, :] = jnp.sum(sum_ref[...] * forms_ref[j].astype(F32), axis=0, keepdims=True)
    charge_ref[...] = lane_sums(rows[...])


def turn_kernel(forms_ref, turned_ref, wide):
    form_count = forms_ref.shape[0]
    for j in range(form_count):
        wide[j * N : (j + 1) * N, :] = forms_ref[j].astype(F32)
    for row in range(N):
        turned_ref[row] = wide[pl.ds(row, form_count, stride=N), :].astype(BF16)


def side_kernel(second, block_ref, factors_ref, partial_ref, next_ref, blocks, products):
    core = lax.rem(lax.axis_index("ka"), CORES)
    far = own_sum_is_even() != second
    flipped = (core == 1) == far
    last = 2 * SPAN
    unpack(rows_of(block_ref), blocks, lambda i: jnp.where(flipped, KL - 1 - i, i))
    factors = [factors_ref.at[jnp.where(flipped, distance, last - distance)] for distance in range(KL)]
    for k in range(0, KL, 2):
        clear_halves(products, k, k + 1)
    for distance in range(KL):
        halves = half_products(blocks, 0, KL - distance, factors[distance][...])
        for k in range(distance, KL):
            place_halves(products, k, distance, halves[(k - distance) * N : (k - distance + 1) * N, :])
    for pair in range(KL // 2):
        result = second_product(products, pair, factors[: 2 * pair + 2])
        for member in range(2):
            k = 2 * pair + member
            k = jnp.where(flipped, KL - 1 - k, k)
            next_ref[k] = partial_ref[k] - result[:, member * N : (member + 1) * N]


def last_kernel(
    even_ref, odd_ref, factors_ref, partial_ref, turned_ref, charge_ref, level_ref, stats_ref,
    blocks, products, diagonals, squares,
):
    flipped = lax.rem(lax.axis_index("ka"), CORES) == 1
    last = 2 * SPAN
    unpack(rows_of_either(own_sum_is_even(), odd_ref, even_ref), blocks, lambda i: jnp.where(flipped, KL - 1 - i, i))
    factors = [factors_ref.at[jnp.where(flipped, last - distance, distance)] for distance in range(CHIP)]
    for k in range(0, KL, 2):
        clear_halves(products, k, 0)
        clear_halves(products, k + 1, KL)
    for distance in range(1, CHIP):
        low = max(0, KL - distance)
        high = min(KL, CHIP - distance)
        halves = half_products(blocks, distance + low - KL, high - low, factors[distance][...])
        for k in range(low, high):
            place_halves(products, k, distance - (KL - 1 - k // 2 * 2), halves[(k - low) * N : (k - low + 1) * N, :])
    row, col = square_iota()
    for pair in range(KL // 2):
        first = KL - 1 - 2 * pair
        result = second_product(products, pair, factors[first : first + KL + 1])
        for member in range(2):
            k = 2 * pair + member
            k = jnp.where(flipped, KL - 1 - k, k)
            combined = partial_ref[k] - result[:, member * N : (member + 1) * N]
            level = 0.5 * (combined + combined.T)
            level_ref[pl.ds(pl.multiple_of(k * N, N), N), :] = level
            diagonals[pl.ds(k, 1), :] = jnp.sum(jnp.where(row == col, level, 0.0), axis=0, keepdims=True)
            outside = jnp.where(row == col, 0.0, level)
            squares[pl.ds(k, 1), :] = jnp.sum(outside * outside, axis=0, keepdims=True)

    mean = jnp.sum(diagonals[...], axis=1, keepdims=True) / N
    rest = diagonals[...] - mean
    norm = jnp.sum(squares[...] + rest * rest, axis=1, keepdims=True)
    form_count = turned_ref.shape[1]
    lane = lax.broadcasted_iota(jnp.int32, (KL, N), 1)
    place = lax.broadcasted_iota(jnp.int32, (KL, N), 0)
    chunk = 16
    dots = jnp.zeros((2 * KL, form_count), F32)
    for start in range(0, N, chunk):
        lefts, rights = [], []
        for at in range(start, start + chunk):
            values = level_ref[pl.ds(at, KL, stride=N), :]
            values = jnp.where(lane == at, values - mean, values)
            high = values.astype(BF16).astype(F32)
            lefts.append(jnp.concatenate([high, values - high], axis=0).astype(BF16))
            rights.append(turned_ref[at])
        dots = dots + lax.dot_general(
            jnp.concatenate(lefts, axis=1), jnp.concatenate(rights, axis=1), LANES_LAST, preferred_element_type=F32
        )
    overlaps = dots[:KL, :] + dots[KL:, :]
    numbers = jnp.where(lane == form_count + place, norm, 0.0)
    numbers = numbers + jnp.where(lane == form_count + KL + place, mean, 0.0)
    charge = jnp.concatenate([charge_ref[0:1, :], jnp.zeros((1, N - form_count), F32)], axis=1)
    numbers = jnp.sum(numbers, axis=0, keepdims=True) + charge
    stats = jnp.concatenate([overlaps[k : k + 1, :] for k in range(KL)] + [numbers], axis=1)
    stats_ref[...] = jnp.broadcast_to(stats, stats_ref.shape)


def final_kernel(
    stats_ref, level_ref, forms_ref, coupling_ref, occupations_ref, fock_hbm, density_hbm, fock, density, sent
):
    form_count = forms_ref.shape[0]
    count = stats_ref.shape[0]
    total = count * KL
    overlap_count = KL * form_count
    charge = jnp.sum(stats_ref[:, overlap_count : overlap_count + form_count], axis=0, keepdims=True) / total
    weights = coupling_ref[...] * charge
    row, col = square_iota()
    hartree = jnp.zeros((N, N), F32)
    for j in range(form_count):
        hartree = hartree + weights[:, j : j + 1] * forms_ref[j].astype(F32)
    hartree = 0.5 * (hartree + hartree.T)
    diagonal = jnp.sum(jnp.where(row == col, hartree, 0.0), axis=0, keepdims=True)
    offset = jnp.sum(diagonal, axis=1, keepdims=True) / N
    beside = jnp.where(row == col, 0.0, hartree)
    own = jnp.sum(beside * beside, axis=0, keepdims=True) + (diagonal - offset) ** 2
    own = jnp.sum(own, axis=1, keepdims=True)
    norms_at = overlap_count + form_count
    means = stats_ref[:, norms_at + KL : norms_at + 2 * KL]
    mean = jnp.sum(means, keepdims=True) / total
    cross = [
        jnp.sum(stats_ref[:, k * form_count : (k + 1) * form_count] * weights, axis=1, keepdims=True)
        for k in range(KL)
    ]
    cross = jnp.concatenate(cross, axis=1)
    norms = stats_ref[:, norms_at : norms_at + KL] + 2.0 * cross + own + N * (means - mean) ** 2
    radius = jnp.sqrt(1e-06 + jnp.max(norms, keepdims=True))
    scale = 0.5 / radius
    shift = offset + mean
    eye = jnp.where(row == col, 1.0, 0.0).astype(F32)
    current = []
    for k in range(KL):
        fock[k] = level_ref[k * N : (k + 1) * N, :] + hartree
        filling = occupations_ref[k].astype(F32) / N - 0.5
        current.append((filling + scale * shift) * eye - scale * fock[k])
    copies = [pltpu.make_async_copy(fock, fock_hbm, sent.at[0])]
    copies[0].start()
    for _ in range(NPUR):
        for k in range(KL):
            short = current[k].astype(BF16)
            square = jnp.dot(short, short, preferred_element_type=F32).astype(BF16)
            cube = jnp.dot(square, short, preferred_element_type=F32)
            current[k] = 1.5 * current[k] - 2.0 * cube
    for k in range(KL):
        density[k] = current[k] + 0.5 * eye
        if k % 2 == 1:
            ready = pl.ds(k - 1, 2)
            copies.append(pltpu.make_async_copy(density.at[ready], density_hbm.at[ready], sent.at[(k + 1) // 2]))
            copies[-1].start()
    for copy in copies:
        copy.wait()


def per_device(density, hamiltonian, occupations, form_factors, hartree_forms, coupling):
    kpoint_count = density.shape[0]
    count = lax.axis_size("ka")
    form_count = hartree_forms.shape[0]
    assert kpoint_count == KL and CHIP == SPAN and count % CORES == 0
    shape = jax.ShapeDtypeStruct
    packed, deviation_sum = pl.pallas_call(
        pack_kernel,
        out_shape=(shape((PACK, N), BF16), shape((N, N), F32)),
        in_specs=[HBM],
        out_specs=(VMEM, VMEM),
        scratch_shapes=[pltpu.VMEM((KL, N, N), F32), pltpu.SemaphoreType.DMA(())],
        compiler_params=params(16),
        cost_estimate=pl.CostEstimate(flops=5 * 10**9, bytes_accessed=2 * 10**6, transcendentals=0),
    )(in_hbm(density))
    across = [(d, d ^ 1) for d in range(count)]
    within = [(d, d ^ CORES) for d in range(count)]
    between = [(d, ((d + CORES) ^ CORES) - CORES) for d in range(count)]
    between = [(d, target % count) for d, target in between]
    other = lax.ppermute(packed, "ka", across)
    even = lax.ppermute(packed, "ka", within)
    again = pl.pallas_call(
        copy_kernel, out_shape=shape((PACK, N), BF16), in_specs=[VMEM], out_specs=VMEM, compiler_params=params(16)
    )(packed)
    odd = lax.ppermute(again, "ka", between)
    partial, charge = pl.pallas_call(
        inner_kernel,
        out_shape=(shape((KL, N, N), F32), shape((8, form_count), F32)),
        in_specs=[VMEM] * 6,
        out_specs=(VMEM, VMEM),
        scratch_shapes=[
            pltpu.VMEM((CHIP, N, N), BF16),
            pltpu.VMEM((KL // 2, (CHIP + 1) * 2 * N, 2 * N), BF16),
            pltpu.VMEM((form_count, N), F32),
        ],
        compiler_params=params(28),
        cost_estimate=pl.CostEstimate(flops=5 * 10**9, bytes_accessed=5 * 10**6, transcendentals=0),
    )(packed, other, form_factors, hamiltonian, deviation_sum, hartree_forms)

    side_cost = pl.CostEstimate(flops=2 * 10**9, bytes_accessed=5 * 10**6, transcendentals=0)

    def side(second, block, partial):
        return pl.pallas_call(
            functools.partial(side_kernel, second),
            out_shape=shape((KL, N, N), F32),
            in_specs=[VMEM] * 3,
            out_specs=VMEM,
            scratch_shapes=[pltpu.VMEM((KL, N, N), BF16), pltpu.VMEM((KL // 2, KL * 2 * N, 2 * N), BF16)],
            compiler_params=params(24),
            cost_estimate=side_cost,
        )(block, form_factors, partial)

    partial, hartree_forms = lax.optimization_barrier((partial, hartree_forms))
    turned = pl.pallas_call(
        turn_kernel,
        out_shape=shape((N, form_count, N), BF16),
        in_specs=[VMEM],
        out_specs=VMEM,
        scratch_shapes=[pltpu.VMEM((form_count * N, N), F32)],
        compiler_params=params(16),
        cost_estimate=side_cost,
    )(hartree_forms)
    partial, turned, even = lax.optimization_barrier((partial, turned, even))
    even_across = lax.ppermute(even, "ka", across)
    partial = side(False, even, partial)
    partial, odd = lax.optimization_barrier((partial, odd))
    odd_across = lax.ppermute(odd, "ka", across)
    partial = side(True, odd, partial)
    level, stats = pl.pallas_call(
        last_kernel,
        out_shape=(shape((KL * N, N), F32), shape((count, KL * form_count + N), F32)),
        in_specs=[VMEM] * 6,
        out_specs=(VMEM, VMEM),
        scratch_shapes=[
            pltpu.VMEM((KL, N, N), BF16),
            pltpu.VMEM((KL // 2, (KL + 1) * 2 * N, 2 * N), BF16),
            pltpu.VMEM((KL, N), F32),
            pltpu.VMEM((KL, N), F32),
        ],
        compiler_params=params(28),
    )(even_across, odd_across, form_factors, partial, turned, charge)
    shared = lax.all_to_all(stats, "ka", 0, 0, tiled=True)
    return pl.pallas_call(
        final_kernel,
        out_shape=(shape((KL, N, N), F32), shape((KL, N, N), F32)),
        in_specs=[VMEM] * 4 + [SMEM],
        out_specs=(HBM, HBM),
        scratch_shapes=[pltpu.VMEM((KL, N, N), F32), pltpu.VMEM((KL, N, N), F32), pltpu.SemaphoreType.DMA((1 + KL // 2,))],
        compiler_params=params(24),
    )(shared, level, hartree_forms, coupling.reshape(1, form_count), occupations)


def solution(mesh):
    placed = (P("ka", None, None), P("ka", None, None), P("ka"), P(), P(), P())
    return jax.shard_map(
        per_device,
        mesh=mesh,
        in_specs=placed,
        out_specs=(P("ka", None, None), P("ka", None, None)),
        check_vma=False,
    )
```

```python
import functools

import jax
import jax.numpy as jnp
from jax import lax
from jax.experimental import pallas as pl
from jax.experimental.pallas import tpu as pltpu
from jax.sharding import PartitionSpec as P

SPAN = 16
NPUR = 6
N = 128
KL = 8
CORES = 2
CHIP = CORES * KL
PACK = KL // 2 * N + 16
SHIFTS = CHIP + KL - 1
F32 = jnp.float32
BF16 = jnp.bfloat16
VMEM = pl.BlockSpec(memory_space=pltpu.VMEM)
SMEM = pl.BlockSpec(memory_space=pltpu.SMEM)
HBM = pl.BlockSpec(memory_space=pltpu.HBM)
LANES_LAST = (((1,), (1,)), ((), ()))


def square_iota():
    row = lax.broadcasted_iota(jnp.int32, (N, N), 0)
    col = lax.broadcasted_iota(jnp.int32, (N, N), 1)
    return row, col


def in_hbm(array):
    return pltpu.with_memory_space_constraint(array, pltpu.HBM)


def params(mib):
    return pltpu.CompilerParams(vmem_limit_bytes=mib << 20)


def lane_sums(rows):
    return lax.dot_general(
        jnp.ones((8, N), F32), rows, LANES_LAST, precision=lax.Precision.HIGHEST, preferred_element_type=F32
    )


def pack_kernel(density_hbm, packed_ref, sum_ref, density, arrived):
    copy = pltpu.make_async_copy(density_hbm, density, arrived)
    copy.start()
    row, col = square_iota()
    half_eye = jnp.where(row == col, 0.5, 0.0).astype(F32)
    total = jnp.zeros((N, N), F32)
    diagonals = []
    copy.wait()
    for pair in range(KL // 2):
        parts = []
        for member in range(2):
            deviation = (density[2 * pair + member] - half_eye).astype(BF16).astype(F32)
            total = total + deviation
            parts.append(0.5 * (deviation + deviation.T))
        packed_ref[pair * N : (pair + 1) * N, :] = jnp.where(row <= col, parts[0], parts[1]).astype(BF16)
        diagonals.append(jnp.sum(jnp.where(row == col, parts[1], 0.0), axis=0, keepdims=True))
    diagonals.append(jnp.zeros((16 - KL // 2, N), F32))
    packed_ref[KL // 2 * N :, :] = jnp.concatenate(diagonals, axis=0).astype(BF16)
    sum_ref[...] = total


def copy_kernel(packed_ref, again_ref):
    again_ref[...] = packed_ref[...]


def unpack(load, blocks, place):
    row, col = square_iota()
    diagonals = load(KL // 2 * N, PACK)
    for pair in range(KL // 2):
        both = load(pair * N, (pair + 1) * N)
        flipped = both.T
        blocks[place(2 * pair)] = jnp.where(row <= col, both, flipped).astype(BF16)
        second = jnp.where(row > col, both, jnp.where(row < col, flipped, diagonals[pair : pair + 1, :]))
        blocks[place(2 * pair + 1)] = second.astype(BF16)


def own_sum_is_even():
    index = lax.axis_index("ka")
    return lax.rem(index // CORES + index, 2) == 0


def rows_of(packed_ref):
    return lambda low, high: packed_ref[low:high, :].astype(F32)


def rows_of_either(choice, first_ref, second_ref):
    return lambda low, high: jnp.where(
        choice, first_ref[low:high, :].astype(F32), second_ref[low:high, :].astype(F32)
    )


def half_products(blocks, first, count, factor):
    left = blocks[first : first + count].reshape(count * N, N)
    return lax.dot_general(left, factor.reshape(2 * N, N), LANES_LAST, preferred_element_type=F32).astype(BF16)


def place_halves(products, k, slot, piece):
    lanes = slice(k % 2 * N, (k % 2 + 1) * N)
    for term in range(2):
        products[k // 2, (2 * slot + term) * N : (2 * slot + term + 1) * N, lanes] = piece[:, term * N : (term + 1) * N]


def clear_halves(products, k, slot):
    lanes = slice(k % 2 * N, (k % 2 + 1) * N)
    products[k // 2, 2 * slot * N : (2 * slot + 2) * N, lanes] = jnp.zeros((2 * N, N), BF16)


def second_product(products, pair, factors):
    left = jnp.concatenate([factor[term] for factor in factors for term in range(2)], axis=1)
    right = products[pair, : 2 * N * len(factors), :]
    return jnp.dot(left, right, preferred_element_type=F32)


def inner_kernel(
    own_ref, other_ref, factors_ref, hamiltonian_ref, sum_ref, forms_ref, partial_ref, charge_ref,
    blocks, products, rows,
):
    core = lax.rem(lax.axis_index("ka"), CORES)
    base = SPAN - (KL - 1) - KL * core
    factors = [factors_ref.at[base + shift] for shift in range(SHIFTS)]
    unpack(rows_of(own_ref), blocks, lambda i: core * KL + i)
    unpack(rows_of(other_ref), blocks, lambda i: (1 - core) * KL + i)
    for k in range(0, KL, 2):
        clear_halves(products, k, 0)
        clear_halves(products, k + 1, CHIP)
    for shift in range(SHIFTS):
        low = max(0, KL - 1 - shift)
        high = min(KL, SHIFTS - shift)
        halves = half_products(blocks, low + shift - (KL - 1), high - low, factors[shift][...])
        for k in range(low, high):
            place_halves(products, k, shift - (KL - 2 - k // 2 * 2), halves[(k - low) * N : (k - low + 1) * N, :])
    for pair in range(KL // 2):
        first = KL - 2 - 2 * pair
        result = second_product(products, pair, factors[first : first + CHIP + 1])
        for member in range(2):
            k = 2 * pair + member
            partial_ref[k] = hamiltonian_ref[k] - result[:, member * N : (member + 1) * N]
    for j in range(forms_ref.shape[0]):
        rows[j : j + 1, :] = jnp.sum(sum_ref[...] * forms_ref[j].astype(F32), axis=0, keepdims=True)
    charge_ref[...] = lane_sums(rows[...])


def turn_kernel(forms_ref, turned_ref, wide):
    form_count = forms_ref.shape[0]
    group = N // turned_ref.shape[0]
    for j in range(form_count):
        wide[j * N : (j + 1) * N, :] = forms_ref[j].astype(F32)
    for at in range(turned_ref.shape[0]):
        rows = [wide[pl.ds(at * group + row, form_count, stride=N), :] for row in range(group)]
        turned_ref[at] = jnp.concatenate(rows, axis=0).T.astype(BF16)


def side_kernel(second, block_ref, factors_ref, partial_ref, next_ref, blocks, products):
    core = lax.rem(lax.axis_index("ka"), CORES)
    far = own_sum_is_even() != second
    flipped = (core == 1) == far
    last = 2 * SPAN
    unpack(rows_of(block_ref), blocks, lambda i: jnp.where(flipped, KL - 1 - i, i))
    factors = [factors_ref.at[jnp.where(flipped, distance, last - distance)] for distance in range(KL)]
    for k in range(0, KL, 2):
        clear_halves(products, k, k + 1)
    for distance in range(KL):
        halves = half_products(blocks, 0, KL - distance, factors[distance][...])
        for k in range(distance, KL):
            place_halves(products, k, distance, halves[(k - distance) * N : (k - distance + 1) * N, :])
    for pair in range(KL // 2):
        result = second_product(products, pair, factors[: 2 * pair + 2])
        for member in range(2):
            k = 2 * pair + member
            k = jnp.where(flipped, KL - 1 - k, k)
            next_ref[k] = partial_ref[k] - result[:, member * N : (member + 1) * N]


def last_kernel(
    even_ref, odd_ref, factors_ref, partial_ref, turned_ref, charge_ref, level_ref, stats_ref,
    blocks, products, diagonals, squares,
):
    flipped = lax.rem(lax.axis_index("ka"), CORES) == 1
    last = 2 * SPAN
    unpack(rows_of_either(own_sum_is_even(), odd_ref, even_ref), blocks, lambda i: jnp.where(flipped, KL - 1 - i, i))
    factors = [factors_ref.at[jnp.where(flipped, last - distance, distance)] for distance in range(CHIP)]
    for k in range(0, KL, 2):
        clear_halves(products, k, 0)
        clear_halves(products, k + 1, KL)
    for distance in range(1, CHIP):
        low = max(0, KL - distance)
        high = min(KL, CHIP - distance)
        halves = half_products(blocks, distance + low - KL, high - low, factors[distance][...])
        for k in range(low, high):
            place_halves(products, k, distance - (KL - 1 - k // 2 * 2), halves[(k - low) * N : (k - low + 1) * N, :])
    row, col = square_iota()
    for pair in range(KL // 2):
        first = KL - 1 - 2 * pair
        result = second_product(products, pair, factors[first : first + KL + 1])
        for member in range(2):
            k = 2 * pair + member
            k = jnp.where(flipped, KL - 1 - k, k)
            combined = partial_ref[k] - result[:, member * N : (member + 1) * N]
            level = 0.5 * (combined + combined.T)
            level_ref[pl.ds(pl.multiple_of(k * N, N), N), :] = level
            diagonals[pl.ds(k, 1), :] = jnp.sum(jnp.where(row == col, level, 0.0), axis=0, keepdims=True)
            outside = jnp.where(row == col, 0.0, level)
            squares[pl.ds(k, 1), :] = jnp.sum(outside * outside, axis=0, keepdims=True)

    mean = jnp.sum(diagonals[...], axis=1, keepdims=True) / N
    rest = diagonals[...] - mean
    norm = jnp.sum(squares[...] + rest * rest, axis=1, keepdims=True)
    lane = lax.broadcasted_iota(jnp.int32, (KL, N), 1)
    place = lax.broadcasted_iota(jnp.int32, (KL, N), 0)
    group = N // turned_ref.shape[0]
    form_count = turned_ref.shape[2] // group
    eye = jnp.where(row == col, 1.0, 0.0).astype(F32)
    table = jnp.zeros((2 * KL * group, group * form_count), F32)
    for at in range(0, N // group, 2):
        lefts = []
        for first in (at * group, (at + 1) * group):
            highs, lows = [], []
            for k in range(KL):
                values = level_ref[k * N + first : k * N + first + group, :]
                values = values - mean[k : k + 1, :] * eye[first : first + group, :]
                highs.append(values.astype(BF16).astype(F32))
                lows.append(values - highs[-1])
            lefts.append(jnp.concatenate(highs + lows, axis=0).astype(BF16))
        table = table + jnp.dot(
            jnp.concatenate(lefts, axis=1), turned_ref[at : at + 2].reshape(2 * N, -1), preferred_element_type=F32
        )
    at_row = lax.broadcasted_iota(jnp.int32, table.shape, 0) % group
    at_lane = lax.broadcasted_iota(jnp.int32, table.shape, 1) // form_count
    table = jnp.where(at_row == at_lane, table, 0.0)
    table = jnp.sum(table.reshape(2 * KL, group, group * form_count), axis=1)
    table = table[:KL, :] + table[KL:, :]
    overlaps = jnp.zeros((KL, form_count), F32)
    for at in range(group):
        overlaps = overlaps + table[:, at * form_count : (at + 1) * form_count]
    numbers = jnp.where(lane == form_count + place, norm, 0.0)
    numbers = numbers + jnp.where(lane == form_count + KL + place, mean, 0.0)
    charge = jnp.concatenate([charge_ref[0:1, :], jnp.zeros((1, N - form_count), F32)], axis=1)
    numbers = jnp.sum(numbers, axis=0, keepdims=True) + charge
    stats = jnp.concatenate([overlaps[k : k + 1, :] for k in range(KL)] + [numbers], axis=1)
    stats_ref[...] = jnp.broadcast_to(stats, stats_ref.shape)


def final_kernel(
    stats_ref, level_ref, forms_ref, coupling_ref, occupations_ref, fock_hbm, density_hbm, fock, density, sent
):
    form_count = forms_ref.shape[0]
    count = stats_ref.shape[0]
    total = count * KL
    overlap_count = KL * form_count
    charge = jnp.sum(stats_ref[:, overlap_count : overlap_count + form_count], axis=0, keepdims=True) / total
    weights = coupling_ref[...] * charge
    row, col = square_iota()
    hartree = jnp.zeros((N, N), F32)
    for j in range(form_count):
        hartree = hartree + weights[:, j : j + 1] * forms_ref[j].astype(F32)
    hartree = 0.5 * (hartree + hartree.T)
    diagonal = jnp.sum(jnp.where(row == col, hartree, 0.0), axis=0, keepdims=True)
    offset = jnp.sum(diagonal, axis=1, keepdims=True) / N
    beside = jnp.where(row == col, 0.0, hartree)
    own = jnp.sum(beside * beside, axis=0, keepdims=True) + (diagonal - offset) ** 2
    own = jnp.sum(own, axis=1, keepdims=True)
    norms_at = overlap_count + form_count
    means = stats_ref[:, norms_at + KL : norms_at + 2 * KL]
    mean = jnp.sum(means, keepdims=True) / total
    cross = [
        jnp.sum(stats_ref[:, k * form_count : (k + 1) * form_count] * weights, axis=1, keepdims=True)
        for k in range(KL)
    ]
    cross = jnp.concatenate(cross, axis=1)
    norms = stats_ref[:, norms_at : norms_at + KL] + 2.0 * cross + own + N * (means - mean) ** 2
    radius = jnp.sqrt(1e-06 + jnp.max(norms, keepdims=True))
    scale = 0.5 / radius
    shift = offset + mean
    eye = jnp.where(row == col, 1.0, 0.0).astype(F32)
    current = []
    for k in range(KL):
        fock[k] = level_ref[k * N : (k + 1) * N, :] + hartree
        filling = occupations_ref[k].astype(F32) / N - 0.5
        current.append((filling + scale * shift) * eye - scale * fock[k])
    copies = [pltpu.make_async_copy(fock, fock_hbm, sent.at[0])]
    copies[0].start()
    for _ in range(NPUR):
        for k in range(KL):
            short = current[k].astype(BF16)
            square = jnp.dot(short, short, preferred_element_type=F32).astype(BF16)
            cube = jnp.dot(square, short, preferred_element_type=F32)
            current[k] = 1.5 * current[k] - 2.0 * cube
    for k in range(KL):
        density[k] = current[k] + 0.5 * eye
        if k % 2 == 1:
            ready = pl.ds(k - 1, 2)
            copies.append(pltpu.make_async_copy(density.at[ready], density_hbm.at[ready], sent.at[(k + 1) // 2]))
            copies[-1].start()
    for copy in copies:
        copy.wait()


def per_device(density, hamiltonian, occupations, form_factors, hartree_forms, coupling):
    kpoint_count = density.shape[0]
    count = lax.axis_size("ka")
    form_count = hartree_forms.shape[0]
    assert kpoint_count == KL and CHIP == SPAN and count % CORES == 0
    shape = jax.ShapeDtypeStruct
    packed, deviation_sum = pl.pallas_call(
        pack_kernel,
        out_shape=(shape((PACK, N), BF16), shape((N, N), F32)),
        in_specs=[HBM],
        out_specs=(VMEM, VMEM),
        scratch_shapes=[pltpu.VMEM((KL, N, N), F32), pltpu.SemaphoreType.DMA(())],
        compiler_params=params(16),
        cost_estimate=pl.CostEstimate(flops=5 * 10**9, bytes_accessed=2 * 10**6, transcendentals=0),
    )(in_hbm(density))
    across = [(d, d ^ 1) for d in range(count)]
    within = [(d, d ^ CORES) for d in range(count)]
    between = [(d, ((d + CORES) ^ CORES) - CORES) for d in range(count)]
    between = [(d, target % count) for d, target in between]
    other = lax.ppermute(packed, "ka", across)
    even = lax.ppermute(packed, "ka", within)
    again = pl.pallas_call(
        copy_kernel, out_shape=shape((PACK, N), BF16), in_specs=[VMEM], out_specs=VMEM, compiler_params=params(16)
    )(packed)
    odd = lax.ppermute(again, "ka", between)
    partial, charge = pl.pallas_call(
        inner_kernel,
        out_shape=(shape((KL, N, N), F32), shape((8, form_count), F32)),
        in_specs=[VMEM] * 6,
        out_specs=(VMEM, VMEM),
        scratch_shapes=[
            pltpu.VMEM((CHIP, N, N), BF16),
            pltpu.VMEM((KL // 2, (CHIP + 1) * 2 * N, 2 * N), BF16),
            pltpu.VMEM((form_count, N), F32),
        ],
        compiler_params=params(28),
        cost_estimate=pl.CostEstimate(flops=5 * 10**9, bytes_accessed=5 * 10**6, transcendentals=0),
    )(packed, other, form_factors, hamiltonian, deviation_sum, hartree_forms)

    side_cost = pl.CostEstimate(flops=2 * 10**9, bytes_accessed=5 * 10**6, transcendentals=0)

    def side(second, block, partial):
        return pl.pallas_call(
            functools.partial(side_kernel, second),
            out_shape=shape((KL, N, N), F32),
            in_specs=[VMEM] * 3,
            out_specs=VMEM,
            scratch_shapes=[pltpu.VMEM((KL, N, N), BF16), pltpu.VMEM((KL // 2, KL * 2 * N, 2 * N), BF16)],
            compiler_params=params(24),
            cost_estimate=side_cost,
        )(block, form_factors, partial)

    partial, hartree_forms = lax.optimization_barrier((partial, hartree_forms))
    turned = pl.pallas_call(
        turn_kernel,
        out_shape=shape((N * form_count // (2 * N), N, 2 * N), BF16),
        in_specs=[VMEM],
        out_specs=VMEM,
        scratch_shapes=[pltpu.VMEM((form_count * N, N), F32)],
        compiler_params=params(16),
        cost_estimate=side_cost,
    )(hartree_forms)
    partial, turned, even = lax.optimization_barrier((partial, turned, even))
    even_across = lax.ppermute(even, "ka", across)
    partial = side(False, even, partial)
    partial, odd = lax.optimization_barrier((partial, odd))
    odd_across = lax.ppermute(odd, "ka", across)
    partial = side(True, odd, partial)
    level, stats = pl.pallas_call(
        last_kernel,
        out_shape=(shape((KL * N, N), F32), shape((count, KL * form_count + N), F32)),
        in_specs=[VMEM] * 6,
        out_specs=(VMEM, VMEM),
        scratch_shapes=[
            pltpu.VMEM((KL, N, N), BF16),
            pltpu.VMEM((KL // 2, (KL + 1) * 2 * N, 2 * N), BF16),
            pltpu.VMEM((KL, N), F32),
            pltpu.VMEM((KL, N), F32),
        ],
        compiler_params=params(28),
    )(even_across, odd_across, form_factors, partial, turned, charge)
    shared = lax.all_to_all(stats, "ka", 0, 0, tiled=True)
    return pl.pallas_call(
        final_kernel,
        out_shape=(shape((KL, N, N), F32), shape((KL, N, N), F32)),
        in_specs=[VMEM] * 4 + [SMEM],
        out_specs=(HBM, HBM),
        scratch_shapes=[pltpu.VMEM((KL, N, N), F32), pltpu.VMEM((KL, N, N), F32), pltpu.SemaphoreType.DMA((1 + KL // 2,))],
        compiler_params=params(24),
    )(shared, level, hartree_forms, coupling.reshape(1, form_count), occupations)


def solution(mesh):
    placed = (P("ka", None, None), P("ka", None, None), P("ka"), P(), P(), P())
    return jax.shard_map(
        per_device,
        mesh=mesh,
        in_specs=placed,
        out_specs=(P("ka", None, None), P("ka", None, None)),
        check_vma=False,
    )
```

```python
import functools

import jax
import jax.numpy as jnp
from jax import lax
from jax.experimental import pallas as pl
from jax.experimental.pallas import tpu as pltpu
from jax.sharding import PartitionSpec as P

SPAN = 16
NPUR = 6
N = 128
KL = 8
CORES = 2
CHIP = CORES * KL
PACK = KL // 2 * N + 16
SHIFTS = CHIP + KL - 1
F32 = jnp.float32
BF16 = jnp.bfloat16
VMEM = pl.BlockSpec(memory_space=pltpu.VMEM)
SMEM = pl.BlockSpec(memory_space=pltpu.SMEM)
HBM = pl.BlockSpec(memory_space=pltpu.HBM)
LANES_LAST = (((1,), (1,)), ((), ()))


def square_iota():
    row = lax.broadcasted_iota(jnp.int32, (N, N), 0)
    col = lax.broadcasted_iota(jnp.int32, (N, N), 1)
    return row, col


def in_hbm(array):
    return pltpu.with_memory_space_constraint(array, pltpu.HBM)


def params(mib):
    return pltpu.CompilerParams(vmem_limit_bytes=mib << 20)


def lane_sums(rows):
    return lax.dot_general(
        jnp.ones((8, N), F32), rows, LANES_LAST, precision=lax.Precision.HIGHEST, preferred_element_type=F32
    )


def pack_kernel(density_hbm, packed_ref, sum_ref, density, arrived):
    copy = pltpu.make_async_copy(density_hbm, density, arrived)
    copy.start()
    row, col = square_iota()
    half_eye = jnp.where(row == col, 0.5, 0.0).astype(F32)
    total = jnp.zeros((N, N), F32)
    diagonals = []
    copy.wait()
    for pair in range(KL // 2):
        parts = []
        for member in range(2):
            deviation = (density[2 * pair + member] - half_eye).astype(BF16).astype(F32)
            total = total + deviation
            parts.append(0.5 * (deviation + deviation.T))
        packed_ref[pair * N : (pair + 1) * N, :] = jnp.where(row <= col, parts[0], parts[1]).astype(BF16)
        diagonals.append(jnp.sum(jnp.where(row == col, parts[1], 0.0), axis=0, keepdims=True))
    diagonals.append(jnp.zeros((16 - KL // 2, N), F32))
    packed_ref[KL // 2 * N :, :] = jnp.concatenate(diagonals, axis=0).astype(BF16)
    sum_ref[...] = total


def copy_kernel(packed_ref, again_ref):
    again_ref[...] = packed_ref[...]


def unpack(load, blocks, place):
    row, col = square_iota()
    diagonals = load(KL // 2 * N, PACK)
    for pair in range(KL // 2):
        both = load(pair * N, (pair + 1) * N)
        flipped = both.T
        blocks[place(2 * pair)] = jnp.where(row <= col, both, flipped).astype(BF16)
        second = jnp.where(row > col, both, jnp.where(row < col, flipped, diagonals[pair : pair + 1, :]))
        blocks[place(2 * pair + 1)] = second.astype(BF16)


def own_sum_is_even():
    index = lax.axis_index("ka")
    return lax.rem(index // CORES + index, 2) == 0


def rows_of(packed_ref):
    return lambda low, high: packed_ref[low:high, :].astype(F32)


def rows_of_either(choice, first_ref, second_ref):
    return lambda low, high: jnp.where(
        choice, first_ref[low:high, :].astype(F32), second_ref[low:high, :].astype(F32)
    )


def half_products(blocks, first, count, factor):
    left = blocks[first : first + count].reshape(count * N, N)
    return lax.dot_general(left, factor.reshape(2 * N, N), LANES_LAST, preferred_element_type=F32).astype(BF16)


def place_halves(products, k, slot, piece):
    lanes = slice(k % 2 * N, (k % 2 + 1) * N)
    for term in range(2):
        products[k // 2, (2 * slot + term) * N : (2 * slot + term + 1) * N, lanes] = piece[:, term * N : (term + 1) * N]


def clear_halves(products, k, slot):
    lanes = slice(k % 2 * N, (k % 2 + 1) * N)
    products[k // 2, 2 * slot * N : (2 * slot + 2) * N, lanes] = jnp.zeros((2 * N, N), BF16)


def second_product(products, pair, factors):
    left = jnp.concatenate([factor[term] for factor in factors for term in range(2)], axis=1)
    right = products[pair, : 2 * N * len(factors), :]
    return jnp.dot(left, right, preferred_element_type=F32)


def inner_kernel(
    own_ref, other_ref, factors_ref, hamiltonian_ref, sum_ref, forms_ref, partial_ref, charge_ref,
    blocks, products, rows,
):
    core = lax.rem(lax.axis_index("ka"), CORES)
    base = SPAN - (KL - 1) - KL * core
    factors = [factors_ref.at[base + shift] for shift in range(SHIFTS)]
    unpack(rows_of(own_ref), blocks, lambda i: core * KL + i)
    unpack(rows_of(other_ref), blocks, lambda i: (1 - core) * KL + i)
    for k in range(0, KL, 2):
        clear_halves(products, k, 0)
        clear_halves(products, k + 1, CHIP)
    for shift in range(SHIFTS):
        low = max(0, KL - 1 - shift)
        high = min(KL, SHIFTS - shift)
        halves = half_products(blocks, low + shift - (KL - 1), high - low, factors[shift][...])
        for k in range(low, high):
            place_halves(products, k, shift - (KL - 2 - k // 2 * 2), halves[(k - low) * N : (k - low + 1) * N, :])
    for pair in range(KL // 2):
        first = KL - 2 - 2 * pair
        result = second_product(products, pair, factors[first : first + CHIP + 1])
        for member in range(2):
            k = 2 * pair + member
            partial_ref[k] = hamiltonian_ref[k] - result[:, member * N : (member + 1) * N]
    for j in range(forms_ref.shape[0]):
        rows[j : j + 1, :] = jnp.sum(sum_ref[...] * forms_ref[j].astype(F32), axis=0, keepdims=True)
    charge_ref[...] = lane_sums(rows[...])


def turn_kernel(forms_ref, turned_ref, traces_ref, wide, rows):
    form_count = forms_ref.shape[0]
    row, col = square_iota()
    group = N // turned_ref.shape[0]
    for j in range(form_count):
        form = forms_ref[j].astype(F32)
        wide[j * N : (j + 1) * N, :] = form
        rows[j : j + 1, :] = jnp.sum(jnp.where(row == col, form, 0.0), axis=0, keepdims=True)
    for at in range(turned_ref.shape[0]):
        parts = [wide[pl.ds(at * group + place, form_count, stride=N), :] for place in range(group)]
        turned_ref[at] = jnp.concatenate(parts, axis=0).T.astype(BF16)
    traces_ref[...] = lane_sums(rows[...])


def side_kernel(second, block_ref, factors_ref, partial_ref, next_ref, blocks, products):
    core = lax.rem(lax.axis_index("ka"), CORES)
    far = own_sum_is_even() != second
    flipped = (core == 1) == far
    last = 2 * SPAN
    unpack(rows_of(block_ref), blocks, lambda i: jnp.where(flipped, KL - 1 - i, i))
    factors = [factors_ref.at[jnp.where(flipped, distance, last - distance)] for distance in range(KL)]
    for k in range(0, KL, 2):
        clear_halves(products, k, k + 1)
    for distance in range(KL):
        halves = half_products(blocks, 0, KL - distance, factors[distance][...])
        for k in range(distance, KL):
            place_halves(products, k, distance, halves[(k - distance) * N : (k - distance + 1) * N, :])
    for pair in range(KL // 2):
        result = second_product(products, pair, factors[: 2 * pair + 2])
        for member in range(2):
            k = 2 * pair + member
            k = jnp.where(flipped, KL - 1 - k, k)
            next_ref[k] = partial_ref[k] - result[:, member * N : (member + 1) * N]


def last_kernel(
    even_ref, odd_ref, factors_ref, partial_ref, turned_ref, traces_ref, charge_ref, level_ref, stats_ref,
    blocks, products, diagonals, squares,
):
    flipped = lax.rem(lax.axis_index("ka"), CORES) == 1
    last = 2 * SPAN
    unpack(rows_of_either(own_sum_is_even(), odd_ref, even_ref), blocks, lambda i: jnp.where(flipped, KL - 1 - i, i))
    factors = [factors_ref.at[jnp.where(flipped, last - distance, distance)] for distance in range(CHIP)]
    for k in range(0, KL, 2):
        clear_halves(products, k, 0)
        clear_halves(products, k + 1, KL)
    for distance in range(1, CHIP):
        low = max(0, KL - distance)
        high = min(KL, CHIP - distance)
        halves = half_products(blocks, distance + low - KL, high - low, factors[distance][...])
        for k in range(low, high):
            place_halves(products, k, distance - (KL - 1 - k // 2 * 2), halves[(k - low) * N : (k - low + 1) * N, :])
    row, col = square_iota()
    for pair in range(KL // 2):
        first = KL - 1 - 2 * pair
        result = second_product(products, pair, factors[first : first + KL + 1])
        for member in range(2):
            k = 2 * pair + member
            k = jnp.where(flipped, KL - 1 - k, k)
            combined = partial_ref[k] - result[:, member * N : (member + 1) * N]
            level = 0.5 * (combined + combined.T)
            level_ref[pl.ds(pl.multiple_of(k * N, N), N), :] = level
            diagonals[pl.ds(k, 1), :] = jnp.sum(jnp.where(row == col, level, 0.0), axis=0, keepdims=True)
            outside = jnp.where(row == col, 0.0, level)
            squares[pl.ds(k, 1), :] = jnp.sum(outside * outside, axis=0, keepdims=True)

    mean = jnp.sum(diagonals[...], axis=1, keepdims=True) / N
    rest = diagonals[...] - mean
    norm = jnp.sum(squares[...] + rest * rest, axis=1, keepdims=True)
    lane = lax.broadcasted_iota(jnp.int32, (KL, N), 1)
    place = lax.broadcasted_iota(jnp.int32, (KL, N), 0)
    group = N // turned_ref.shape[0]
    form_count = turned_ref.shape[2] // group
    table = jnp.zeros((2 * KL * group, group * form_count), F32)
    for at in range(0, N // group, 2):
        lefts = []
        for first in (at * group, (at + 1) * group):
            highs, lows = [], []
            for k in range(KL):
                values = level_ref[k * N + first : k * N + first + group, :]
                highs.append(values.astype(BF16).astype(F32))
                lows.append(values - highs[-1])
            lefts.append(jnp.concatenate(highs + lows, axis=0).astype(BF16))
        table = table + jnp.dot(
            jnp.concatenate(lefts, axis=1), turned_ref[at : at + 2].reshape(2 * N, -1), preferred_element_type=F32
        )
    at_row = lax.broadcasted_iota(jnp.int32, table.shape, 0) % group
    at_lane = lax.broadcasted_iota(jnp.int32, table.shape, 1) // form_count
    table = jnp.where(at_row == at_lane, table, 0.0)
    table = jnp.sum(table.reshape(2 * KL, group, group * form_count), axis=1)
    table = table[:KL, :] + table[KL:, :]
    overlaps = jnp.zeros((KL, form_count), F32)
    for at in range(group):
        overlaps = overlaps + table[:, at * form_count : (at + 1) * form_count]
    overlaps = overlaps - mean * traces_ref[0:1, :]
    numbers = jnp.where(lane == form_count + place, norm, 0.0)
    numbers = numbers + jnp.where(lane == form_count + KL + place, mean, 0.0)
    charge = jnp.concatenate([charge_ref[0:1, :], jnp.zeros((1, N - form_count), F32)], axis=1)
    numbers = jnp.sum(numbers, axis=0, keepdims=True) + charge
    stats = jnp.concatenate([overlaps[k : k + 1, :] for k in range(KL)] + [numbers], axis=1)
    stats_ref[...] = jnp.broadcast_to(stats, stats_ref.shape)


def final_kernel(
    stats_ref, level_ref, forms_ref, coupling_ref, occupations_ref, fock_hbm, density_hbm, fock, density, sent
):
    form_count = forms_ref.shape[0]
    count = stats_ref.shape[0]
    total = count * KL
    overlap_count = KL * form_count
    charge = jnp.sum(stats_ref[:, overlap_count : overlap_count + form_count], axis=0, keepdims=True) / total
    weights = coupling_ref[...] * charge
    row, col = square_iota()
    hartree = jnp.zeros((N, N), F32)
    for j in range(form_count):
        hartree = hartree + weights[:, j : j + 1] * forms_ref[j].astype(F32)
    hartree = 0.5 * (hartree + hartree.T)
    diagonal = jnp.sum(jnp.where(row == col, hartree, 0.0), axis=0, keepdims=True)
    offset = jnp.sum(diagonal, axis=1, keepdims=True) / N
    beside = jnp.where(row == col, 0.0, hartree)
    own = jnp.sum(beside * beside, axis=0, keepdims=True) + (diagonal - offset) ** 2
    own = jnp.sum(own, axis=1, keepdims=True)
    norms_at = overlap_count + form_count
    means = stats_ref[:, norms_at + KL : norms_at + 2 * KL]
    mean = jnp.sum(means, keepdims=True) / total
    cross = [
        jnp.sum(stats_ref[:, k * form_count : (k + 1) * form_count] * weights, axis=1, keepdims=True)
        for k in range(KL)
    ]
    cross = jnp.concatenate(cross, axis=1)
    norms = stats_ref[:, norms_at : norms_at + KL] + 2.0 * cross + own + N * (means - mean) ** 2
    radius = jnp.sqrt(1e-06 + jnp.max(norms, keepdims=True))
    scale = 0.5 / radius
    shift = offset + mean
    eye = jnp.where(row == col, 1.0, 0.0).astype(F32)
    current = []
    for k in range(KL):
        fock[k] = level_ref[k * N : (k + 1) * N, :] + hartree
        filling = occupations_ref[k].astype(F32) / N - 0.5
        current.append((filling + scale * shift) * eye - scale * fock[k])
    copies = [pltpu.make_async_copy(fock, fock_hbm, sent.at[0])]
    copies[0].start()
    for _ in range(NPUR):
        for k in range(KL):
            short = current[k].astype(BF16)
            square = jnp.dot(short, short, preferred_element_type=F32).astype(BF16)
            cube = jnp.dot(square, short, preferred_element_type=F32)
            current[k] = 1.5 * current[k] - 2.0 * cube
    for k in range(KL):
        density[k] = current[k] + 0.5 * eye
        if k % 2 == 1:
            ready = pl.ds(k - 1, 2)
            copies.append(pltpu.make_async_copy(density.at[ready], density_hbm.at[ready], sent.at[(k + 1) // 2]))
            copies[-1].start()
    for copy in copies:
        copy.wait()


def per_device(density, hamiltonian, occupations, form_factors, hartree_forms, coupling):
    kpoint_count = density.shape[0]
    count = lax.axis_size("ka")
    form_count = hartree_forms.shape[0]
    assert kpoint_count == KL and CHIP == SPAN and count % CORES == 0
    shape = jax.ShapeDtypeStruct
    packed, deviation_sum = pl.pallas_call(
        pack_kernel,
        out_shape=(shape((PACK, N), BF16), shape((N, N), F32)),
        in_specs=[HBM],
        out_specs=(VMEM, VMEM),
        scratch_shapes=[pltpu.VMEM((KL, N, N), F32), pltpu.SemaphoreType.DMA(())],
        compiler_params=params(16),
        cost_estimate=pl.CostEstimate(flops=5 * 10**9, bytes_accessed=2 * 10**6, transcendentals=0),
    )(in_hbm(density))
    across = [(d, d ^ 1) for d in range(count)]
    within = [(d, d ^ CORES) for d in range(count)]
    between = [(d, ((d + CORES) ^ CORES) - CORES) for d in range(count)]
    between = [(d, target % count) for d, target in between]
    other = lax.ppermute(packed, "ka", across)
    even = lax.ppermute(packed, "ka", within)
    again = pl.pallas_call(
        copy_kernel, out_shape=shape((PACK, N), BF16), in_specs=[VMEM], out_specs=VMEM, compiler_params=params(16)
    )(packed)
    odd = lax.ppermute(again, "ka", between)
    partial, charge = pl.pallas_call(
        inner_kernel,
        out_shape=(shape((KL, N, N), F32), shape((8, form_count), F32)),
        in_specs=[VMEM] * 6,
        out_specs=(VMEM, VMEM),
        scratch_shapes=[
            pltpu.VMEM((CHIP, N, N), BF16),
            pltpu.VMEM((KL // 2, (CHIP + 1) * 2 * N, 2 * N), BF16),
            pltpu.VMEM((form_count, N), F32),
        ],
        compiler_params=params(28),
        cost_estimate=pl.CostEstimate(flops=5 * 10**9, bytes_accessed=5 * 10**6, transcendentals=0),
    )(packed, other, form_factors, hamiltonian, deviation_sum, hartree_forms)

    side_cost = pl.CostEstimate(flops=2 * 10**9, bytes_accessed=5 * 10**6, transcendentals=0)

    def side(second, block, partial):
        return pl.pallas_call(
            functools.partial(side_kernel, second),
            out_shape=shape((KL, N, N), F32),
            in_specs=[VMEM] * 3,
            out_specs=VMEM,
            scratch_shapes=[pltpu.VMEM((KL, N, N), BF16), pltpu.VMEM((KL // 2, KL * 2 * N, 2 * N), BF16)],
            compiler_params=params(24),
            cost_estimate=side_cost,
        )(block, form_factors, partial)

    partial, hartree_forms = lax.optimization_barrier((partial, hartree_forms))
    turned, traces = pl.pallas_call(
        turn_kernel,
        out_shape=(shape((N * form_count // (2 * N), N, 2 * N), BF16), shape((8, form_count), F32)),
        in_specs=[VMEM],
        out_specs=(VMEM, VMEM),
        scratch_shapes=[pltpu.VMEM((form_count * N, N), F32), pltpu.VMEM((form_count, N), F32)],
        compiler_params=params(16),
        cost_estimate=side_cost,
    )(hartree_forms)
    partial, turned, even = lax.optimization_barrier((partial, turned, even))
    even_across = lax.ppermute(even, "ka", across)
    partial = side(False, even, partial)
    partial, odd = lax.optimization_barrier((partial, odd))
    odd_across = lax.ppermute(odd, "ka", across)
    partial = side(True, odd, partial)
    level, stats = pl.pallas_call(
        last_kernel,
        out_shape=(shape((KL * N, N), F32), shape((count, KL * form_count + N), F32)),
        in_specs=[VMEM] * 7,
        out_specs=(VMEM, VMEM),
        scratch_shapes=[
            pltpu.VMEM((KL, N, N), BF16),
            pltpu.VMEM((KL // 2, (KL + 1) * 2 * N, 2 * N), BF16),
            pltpu.VMEM((KL, N), F32),
            pltpu.VMEM((KL, N), F32),
        ],
        compiler_params=params(28),
    )(even_across, odd_across, form_factors, partial, turned, traces, charge)
    shared = lax.all_to_all(stats, "ka", 0, 0, tiled=True)
    return pl.pallas_call(
        final_kernel,
        out_shape=(shape((KL, N, N), F32), shape((KL, N, N), F32)),
        in_specs=[VMEM] * 4 + [SMEM],
        out_specs=(HBM, HBM),
        scratch_shapes=[pltpu.VMEM((KL, N, N), F32), pltpu.VMEM((KL, N, N), F32), pltpu.SemaphoreType.DMA((1 + KL // 2,))],
        compiler_params=params(24),
    )(shared, level, hartree_forms, coupling.reshape(1, form_count), occupations)


def solution(mesh):
    placed = (P("ka", None, None), P("ka", None, None), P("ka"), P(), P(), P())
    return jax.shard_map(
        per_device,
        mesh=mesh,
        in_specs=placed,
        out_specs=(P("ka", None, None), P("ka", None, None)),
        check_vma=False,
    )
```

```python
import functools

import jax
import jax.numpy as jnp
from jax import lax
from jax.experimental import pallas as pl
from jax.experimental.pallas import tpu as pltpu
from jax.sharding import PartitionSpec as P

SPAN = 16
NPUR = 6
N = 128
KL = 8
CORES = 2
CHIP = CORES * KL
PACK = KL // 2 * N + 16
SHIFTS = CHIP + KL - 1
F32 = jnp.float32
BF16 = jnp.bfloat16
VMEM = pl.BlockSpec(memory_space=pltpu.VMEM)
SMEM = pl.BlockSpec(memory_space=pltpu.SMEM)
HBM = pl.BlockSpec(memory_space=pltpu.HBM)
LANES_LAST = (((1,), (1,)), ((), ()))


def square_iota():
    row = lax.broadcasted_iota(jnp.int32, (N, N), 0)
    col = lax.broadcasted_iota(jnp.int32, (N, N), 1)
    return row, col


def in_hbm(array):
    return pltpu.with_memory_space_constraint(array, pltpu.HBM)


def params(mib):
    return pltpu.CompilerParams(vmem_limit_bytes=mib << 20)


def lane_sums(rows):
    return lax.dot_general(
        jnp.ones((8, N), F32), rows, LANES_LAST, precision=lax.Precision.HIGHEST, preferred_element_type=F32
    )


def pack_kernel(density_hbm, packed_ref, sum_ref, density, arrived):
    copy = pltpu.make_async_copy(density_hbm, density, arrived)
    copy.start()
    row, col = square_iota()
    half_eye = jnp.where(row == col, 0.5, 0.0).astype(F32)
    total = jnp.zeros((N, N), F32)
    diagonals = []
    copy.wait()
    for pair in range(KL // 2):
        parts = []
        for member in range(2):
            deviation = (density[2 * pair + member] - half_eye).astype(BF16).astype(F32)
            total = total + deviation
            parts.append(0.5 * (deviation + deviation.T))
        packed_ref[pair * N : (pair + 1) * N, :] = jnp.where(row <= col, parts[0], parts[1]).astype(BF16)
        diagonals.append(jnp.sum(jnp.where(row == col, parts[1], 0.0), axis=0, keepdims=True))
    diagonals.append(jnp.zeros((16 - KL // 2, N), F32))
    packed_ref[KL // 2 * N :, :] = jnp.concatenate(diagonals, axis=0).astype(BF16)
    sum_ref[...] = total


def copy_kernel(packed_ref, again_ref):
    again_ref[...] = packed_ref[...]


def unpack(load, blocks, place):
    row, col = square_iota()
    diagonals = load(KL // 2 * N, PACK)
    for pair in range(KL // 2):
        both = load(pair * N, (pair + 1) * N)
        flipped = both.T
        blocks[place(2 * pair)] = jnp.where(row <= col, both, flipped).astype(BF16)
        second = jnp.where(row > col, both, jnp.where(row < col, flipped, diagonals[pair : pair + 1, :]))
        blocks[place(2 * pair + 1)] = second.astype(BF16)


def own_sum_is_even():
    index = lax.axis_index("ka")
    return lax.rem(index // CORES + index, 2) == 0


def rows_of(packed_ref):
    return lambda low, high: packed_ref[low:high, :].astype(F32)


def rows_of_either(choice, first_ref, second_ref):
    return lambda low, high: jnp.where(
        choice, first_ref[low:high, :].astype(F32), second_ref[low:high, :].astype(F32)
    )


def half_products(blocks, first, count, factor):
    left = blocks[first : first + count].reshape(count * N, N)
    return lax.dot_general(left, factor.reshape(2 * N, N), LANES_LAST, preferred_element_type=F32).astype(BF16)


def place_halves(products, k, slot, piece):
    lanes = slice(k % 2 * N, (k % 2 + 1) * N)
    for term in range(2):
        products[k // 2, (2 * slot + term) * N : (2 * slot + term + 1) * N, lanes] = piece[:, term * N : (term + 1) * N]


def clear_halves(products, k, slot):
    lanes = slice(k % 2 * N, (k % 2 + 1) * N)
    products[k // 2, 2 * slot * N : (2 * slot + 2) * N, lanes] = jnp.zeros((2 * N, N), BF16)


def second_product(products, pair, factors):
    left = jnp.concatenate([factor[term] for factor in factors for term in range(2)], axis=1)
    right = products[pair, : 2 * N * len(factors), :]
    return jnp.dot(left, right, preferred_element_type=F32)


def inner_kernel(
    own_ref, other_ref, factors_ref, hamiltonian_ref, sum_ref, forms_ref, partial_ref, charge_ref,
    blocks, products, rows,
):
    core = lax.rem(lax.axis_index("ka"), CORES)
    base = SPAN - (KL - 1) - KL * core
    factors = [factors_ref.at[base + shift] for shift in range(SHIFTS)]
    unpack(rows_of(own_ref), blocks, lambda i: core * KL + i)
    unpack(rows_of(other_ref), blocks, lambda i: (1 - core) * KL + i)
    for k in range(0, KL, 2):
        clear_halves(products, k, 0)
        clear_halves(products, k + 1, CHIP)
    for shift in range(SHIFTS):
        low = max(0, KL - 1 - shift)
        high = min(KL, SHIFTS - shift)
        halves = half_products(blocks, low + shift - (KL - 1), high - low, factors[shift][...])
        for k in range(low, high):
            place_halves(products, k, shift - (KL - 2 - k // 2 * 2), halves[(k - low) * N : (k - low + 1) * N, :])
    for pair in range(KL // 2):
        first = KL - 2 - 2 * pair
        result = second_product(products, pair, factors[first : first + CHIP + 1])
        for member in range(2):
            k = 2 * pair + member
            partial_ref[k] = hamiltonian_ref[k] - result[:, member * N : (member + 1) * N]
    for j in range(forms_ref.shape[0]):
        rows[j : j + 1, :] = jnp.sum(sum_ref[...] * forms_ref[j].astype(F32), axis=0, keepdims=True)
    charge_ref[...] = lane_sums(rows[...])


def turn_kernel(forms_ref, turned_ref):
    group = N // turned_ref.shape[0]
    for at in range(0, turned_ref.shape[0], 2):
        rows = forms_ref[:, at * group : (at + 2) * group, :].astype(F32)
        for half in range(2):
            part = rows[:, half * group : (half + 1) * group, :]
            turned_ref[at + half] = part.reshape(-1, N).T.astype(BF16)


def side_kernel(second, block_ref, factors_ref, partial_ref, next_ref, blocks, products):
    core = lax.rem(lax.axis_index("ka"), CORES)
    far = own_sum_is_even() != second
    flipped = (core == 1) == far
    last = 2 * SPAN
    unpack(rows_of(block_ref), blocks, lambda i: jnp.where(flipped, KL - 1 - i, i))
    factors = [factors_ref.at[jnp.where(flipped, distance, last - distance)] for distance in range(KL)]
    for k in range(0, KL, 2):
        clear_halves(products, k, k + 1)
    for distance in range(KL):
        halves = half_products(blocks, 0, KL - distance, factors[distance][...])
        for k in range(distance, KL):
            place_halves(products, k, distance, halves[(k - distance) * N : (k - distance + 1) * N, :])
    for pair in range(KL // 2):
        result = second_product(products, pair, factors[: 2 * pair + 2])
        for member in range(2):
            k = 2 * pair + member
            k = jnp.where(flipped, KL - 1 - k, k)
            next_ref[k] = partial_ref[k] - result[:, member * N : (member + 1) * N]


def last_kernel(
    even_ref, odd_ref, factors_ref, partial_ref, turned_ref, charge_ref, level_ref, stats_ref,
    blocks, products, diagonals, squares,
):
    flipped = lax.rem(lax.axis_index("ka"), CORES) == 1
    last = 2 * SPAN
    unpack(rows_of_either(own_sum_is_even(), odd_ref, even_ref), blocks, lambda i: jnp.where(flipped, KL - 1 - i, i))
    factors = [factors_ref.at[jnp.where(flipped, last - distance, distance)] for distance in range(CHIP)]
    for k in range(0, KL, 2):
        clear_halves(products, k, 0)
        clear_halves(products, k + 1, KL)
    for distance in range(1, CHIP):
        low = max(0, KL - distance)
        high = min(KL, CHIP - distance)
        halves = half_products(blocks, distance + low - KL, high - low, factors[distance][...])
        for k in range(low, high):
            place_halves(products, k, distance - (KL - 1 - k // 2 * 2), halves[(k - low) * N : (k - low + 1) * N, :])
    row, col = square_iota()
    for pair in range(KL // 2):
        first = KL - 1 - 2 * pair
        result = second_product(products, pair, factors[first : first + KL + 1])
        for member in range(2):
            k = 2 * pair + member
            k = jnp.where(flipped, KL - 1 - k, k)
            combined = partial_ref[k] - result[:, member * N : (member + 1) * N]
            level = 0.5 * (combined + combined.T)
            level_ref[pl.ds(pl.multiple_of(k * N, N), N), :] = level
            diagonals[pl.ds(k, 1), :] = jnp.sum(jnp.where(row == col, level, 0.0), axis=0, keepdims=True)
            outside = jnp.where(row == col, 0.0, level)
            squares[pl.ds(k, 1), :] = jnp.sum(outside * outside, axis=0, keepdims=True)

    mean = jnp.sum(diagonals[...], axis=1, keepdims=True) / N
    rest = diagonals[...] - mean
    norm = jnp.sum(squares[...] + rest * rest, axis=1, keepdims=True)
    lane = lax.broadcasted_iota(jnp.int32, (KL, N), 1)
    place = lax.broadcasted_iota(jnp.int32, (KL, N), 0)
    group = N // turned_ref.shape[0]
    form_count = turned_ref.shape[2] // group
    eye = jnp.where(row == col, 1.0, 0.0).astype(F32)
    table = jnp.zeros((2 * KL * group, group * form_count), F32)
    for at in range(0, N // group, 2):
        lefts = []
        for first in (at * group, (at + 1) * group):
            highs, lows = [], []
            for k in range(KL):
                values = level_ref[k * N + first : k * N + first + group, :]
                values = values - mean[k : k + 1, :] * eye[first : first + group, :]
                highs.append(values.astype(BF16).astype(F32))
                lows.append(values - highs[-1])
            lefts.append(jnp.concatenate(highs + lows, axis=0).astype(BF16))
        table = table + jnp.dot(
            jnp.concatenate(lefts, axis=1), turned_ref[at : at + 2].reshape(2 * N, -1), preferred_element_type=F32
        )
    at_row = lax.broadcasted_iota(jnp.int32, table.shape, 0) % group
    at_lane = lax.broadcasted_iota(jnp.int32, table.shape, 1) % group
    table = jnp.where(at_row == at_lane, table, 0.0)
    table = jnp.sum(table.reshape(2 * KL, group, group * form_count), axis=1)
    table = table[:KL, :] + table[KL:, :]
    high = table.astype(BF16)
    low = (table - high.astype(F32)).astype(BF16)
    of_form = lax.broadcasted_iota(jnp.int32, (2 * group * form_count, form_count), 0) // group % form_count
    ones = lax.broadcasted_iota(jnp.int32, of_form.shape, 1) == of_form
    overlaps = jnp.dot(
        jnp.concatenate([high, low], axis=1), jnp.where(ones, 1.0, 0.0).astype(BF16), preferred_element_type=F32
    )
    numbers = jnp.where(lane == form_count + place, norm, 0.0)
    numbers = numbers + jnp.where(lane == form_count + KL + place, mean, 0.0)
    charge = jnp.concatenate([charge_ref[0:1, :], jnp.zeros((1, N - form_count), F32)], axis=1)
    numbers = jnp.sum(numbers, axis=0, keepdims=True) + charge
    stats = jnp.concatenate([overlaps[k : k + 1, :] for k in range(KL)] + [numbers], axis=1)
    stats_ref[...] = jnp.broadcast_to(stats, stats_ref.shape)


def final_kernel(
    stats_ref, level_ref, forms_ref, coupling_ref, occupations_ref, fock_hbm, density_hbm, fock, density, sent
):
    form_count = forms_ref.shape[0]
    count = stats_ref.shape[0]
    total = count * KL
    overlap_count = KL * form_count
    charge = jnp.sum(stats_ref[:, overlap_count : overlap_count + form_count], axis=0, keepdims=True) / total
    weights = coupling_ref[...] * charge
    row, col = square_iota()
    hartree = jnp.zeros((N, N), F32)
    for j in range(form_count):
        hartree = hartree + weights[:, j : j + 1] * forms_ref[j].astype(F32)
    hartree = 0.5 * (hartree + hartree.T)
    diagonal = jnp.sum(jnp.where(row == col, hartree, 0.0), axis=0, keepdims=True)
    offset = jnp.sum(diagonal, axis=1, keepdims=True) / N
    beside = jnp.where(row == col, 0.0, hartree)
    own = jnp.sum(beside * beside, axis=0, keepdims=True) + (diagonal - offset) ** 2
    own = jnp.sum(own, axis=1, keepdims=True)
    norms_at = overlap_count + form_count
    means = stats_ref[:, norms_at + KL : norms_at + 2 * KL]
    mean = jnp.sum(means, keepdims=True) / total
    cross = [
        jnp.sum(stats_ref[:, k * form_count : (k + 1) * form_count] * weights, axis=1, keepdims=True)
        for k in range(KL)
    ]
    cross = jnp.concatenate(cross, axis=1)
    norms = stats_ref[:, norms_at : norms_at + KL] + 2.0 * cross + own + N * (means - mean) ** 2
    radius = jnp.sqrt(1e-06 + jnp.max(norms, keepdims=True))
    scale = 0.5 / radius
    shift = offset + mean
    eye = jnp.where(row == col, 1.0, 0.0).astype(F32)
    current = []
    for k in range(KL):
        fock[k] = level_ref[k * N : (k + 1) * N, :] + hartree
        filling = occupations_ref[k].astype(F32) / N - 0.5
        current.append((filling + scale * shift) * eye - scale * fock[k])
    copies = [pltpu.make_async_copy(fock, fock_hbm, sent.at[0])]
    copies[0].start()
    for _ in range(NPUR):
        for k in range(KL):
            short = current[k].astype(BF16)
            square = jnp.dot(short, short, preferred_element_type=F32).astype(BF16)
            cube = jnp.dot(square, short, preferred_element_type=F32)
            current[k] = 1.5 * current[k] - 2.0 * cube
    for k in range(KL):
        density[k] = current[k] + 0.5 * eye
        if k % 2 == 1:
            ready = pl.ds(k - 1, 2)
            copies.append(pltpu.make_async_copy(density.at[ready], density_hbm.at[ready], sent.at[(k + 1) // 2]))
            copies[-1].start()
    for copy in copies:
        copy.wait()


def per_device(density, hamiltonian, occupations, form_factors, hartree_forms, coupling):
    kpoint_count = density.shape[0]
    count = lax.axis_size("ka")
    form_count = hartree_forms.shape[0]
    assert kpoint_count == KL and CHIP == SPAN and count % CORES == 0
    shape = jax.ShapeDtypeStruct
    packed, deviation_sum = pl.pallas_call(
        pack_kernel,
        out_shape=(shape((PACK, N), BF16), shape((N, N), F32)),
        in_specs=[HBM],
        out_specs=(VMEM, VMEM),
        scratch_shapes=[pltpu.VMEM((KL, N, N), F32), pltpu.SemaphoreType.DMA(())],
        compiler_params=params(16),
        cost_estimate=pl.CostEstimate(flops=5 * 10**9, bytes_accessed=2 * 10**6, transcendentals=0),
    )(in_hbm(density))
    across = [(d, d ^ 1) for d in range(count)]
    within = [(d, d ^ CORES) for d in range(count)]
    between = [(d, ((d + CORES) ^ CORES) - CORES) for d in range(count)]
    between = [(d, target % count) for d, target in between]
    other = lax.ppermute(packed, "ka", across)
    even = lax.ppermute(packed, "ka", within)
    again = pl.pallas_call(
        copy_kernel, out_shape=shape((PACK, N), BF16), in_specs=[VMEM], out_specs=VMEM, compiler_params=params(16)
    )(packed)
    odd = lax.ppermute(again, "ka", between)
    partial, charge = pl.pallas_call(
        inner_kernel,
        out_shape=(shape((KL, N, N), F32), shape((8, form_count), F32)),
        in_specs=[VMEM] * 6,
        out_specs=(VMEM, VMEM),
        scratch_shapes=[
            pltpu.VMEM((CHIP, N, N), BF16),
            pltpu.VMEM((KL // 2, (CHIP + 1) * 2 * N, 2 * N), BF16),
            pltpu.VMEM((form_count, N), F32),
        ],
        compiler_params=params(28),
        cost_estimate=pl.CostEstimate(flops=5 * 10**9, bytes_accessed=5 * 10**6, transcendentals=0),
    )(packed, other, form_factors, hamiltonian, deviation_sum, hartree_forms)

    side_cost = pl.CostEstimate(flops=2 * 10**9, bytes_accessed=5 * 10**6, transcendentals=0)

    def side(second, block, partial):
        return pl.pallas_call(
            functools.partial(side_kernel, second),
            out_shape=shape((KL, N, N), F32),
            in_specs=[VMEM] * 3,
            out_specs=VMEM,
            scratch_shapes=[pltpu.VMEM((KL, N, N), BF16), pltpu.VMEM((KL // 2, KL * 2 * N, 2 * N), BF16)],
            compiler_params=params(24),
            cost_estimate=side_cost,
        )(block, form_factors, partial)

    partial, hartree_forms = lax.optimization_barrier((partial, hartree_forms))
    turned = pl.pallas_call(
        turn_kernel,
        out_shape=shape((N * form_count // (2 * N), N, 2 * N), BF16),
        in_specs=[VMEM],
        out_specs=VMEM,
        compiler_params=params(16),
        cost_estimate=side_cost,
    )(hartree_forms)
    partial, turned, even = lax.optimization_barrier((partial, turned, even))
    even_across = lax.ppermute(even, "ka", across)
    partial = side(False, even, partial)
    partial, odd = lax.optimization_barrier((partial, odd))
    odd_across = lax.ppermute(odd, "ka", across)
    partial = side(True, odd, partial)
    level, stats = pl.pallas_call(
        last_kernel,
        out_shape=(shape((KL * N, N), F32), shape((count, KL * form_count + N), F32)),
        in_specs=[VMEM] * 6,
        out_specs=(VMEM, VMEM),
        scratch_shapes=[
            pltpu.VMEM((KL, N, N), BF16),
            pltpu.VMEM((KL // 2, (KL + 1) * 2 * N, 2 * N), BF16),
            pltpu.VMEM((KL, N), F32),
            pltpu.VMEM((KL, N), F32),
        ],
        compiler_params=params(28),
    )(even_across, odd_across, form_factors, partial, turned, charge)
    shared = lax.all_to_all(stats, "ka", 0, 0, tiled=True)
    return pl.pallas_call(
        final_kernel,
        out_shape=(shape((KL, N, N), F32), shape((KL, N, N), F32)),
        in_specs=[VMEM] * 4 + [SMEM],
        out_specs=(HBM, HBM),
        scratch_shapes=[pltpu.VMEM((KL, N, N), F32), pltpu.VMEM((KL, N, N), F32), pltpu.SemaphoreType.DMA((1 + KL // 2,))],
        compiler_params=params(24),
    )(shared, level, hartree_forms, coupling.reshape(1, form_count), occupations)


def solution(mesh):
    placed = (P("ka", None, None), P("ka", None, None), P("ka"), P(), P(), P())
    return jax.shard_map(
        per_device,
        mesh=mesh,
        in_specs=placed,
        out_specs=(P("ka", None, None), P("ka", None, None)),
        check_vma=False,
    )
```

```python
import functools

import jax
import jax.numpy as jnp
from jax import lax
from jax.experimental import pallas as pl
from jax.experimental.pallas import tpu as pltpu
from jax.sharding import PartitionSpec as P

SPAN = 16
NPUR = 6
N = 128
KL = 8
CORES = 2
CHIP = CORES * KL
PACK = KL // 2 * N + 16
SHIFTS = CHIP + KL - 1
F32 = jnp.float32
BF16 = jnp.bfloat16
VMEM = pl.BlockSpec(memory_space=pltpu.VMEM)
SMEM = pl.BlockSpec(memory_space=pltpu.SMEM)
HBM = pl.BlockSpec(memory_space=pltpu.HBM)
LANES_LAST = (((1,), (1,)), ((), ()))


def square_iota():
    row = lax.broadcasted_iota(jnp.int32, (N, N), 0)
    col = lax.broadcasted_iota(jnp.int32, (N, N), 1)
    return row, col


def in_hbm(array):
    return pltpu.with_memory_space_constraint(array, pltpu.HBM)


def params(mib):
    return pltpu.CompilerParams(vmem_limit_bytes=mib << 20)


def lane_sums(rows):
    return lax.dot_general(
        jnp.ones((8, N), F32), rows, LANES_LAST, precision=lax.Precision.HIGHEST, preferred_element_type=F32
    )


def pack_kernel(density_hbm, packed_ref, sum_ref, density, arrived):
    copy = pltpu.make_async_copy(density_hbm, density, arrived)
    copy.start()
    row, col = square_iota()
    half_eye = jnp.where(row == col, 0.5, 0.0).astype(F32)
    total = jnp.zeros((N, N), F32)
    diagonals = []
    copy.wait()
    for pair in range(KL // 2):
        parts = []
        for member in range(2):
            deviation = (density[2 * pair + member] - half_eye).astype(BF16).astype(F32)
            total = total + deviation
            parts.append(0.5 * (deviation + deviation.T))
        packed_ref[pair * N : (pair + 1) * N, :] = jnp.where(row <= col, parts[0], parts[1]).astype(BF16)
        diagonals.append(jnp.sum(jnp.where(row == col, parts[1], 0.0), axis=0, keepdims=True))
    diagonals.append(jnp.zeros((16 - KL // 2, N), F32))
    packed_ref[KL // 2 * N :, :] = jnp.concatenate(diagonals, axis=0).astype(BF16)
    sum_ref[...] = total


def copy_kernel(packed_ref, again_ref):
    again_ref[...] = packed_ref[...]


def unpack(load, blocks, place):
    row, col = square_iota()
    diagonals = load(KL // 2 * N, PACK)
    for pair in range(KL // 2):
        both = load(pair * N, (pair + 1) * N)
        flipped = both.T
        blocks[place(2 * pair)] = jnp.where(row <= col, both, flipped).astype(BF16)
        second = jnp.where(row > col, both, jnp.where(row < col, flipped, diagonals[pair : pair + 1, :]))
        blocks[place(2 * pair + 1)] = second.astype(BF16)


def own_sum_is_even():
    index = lax.axis_index("ka")
    return lax.rem(index // CORES + index, 2) == 0


def rows_of(packed_ref):
    return lambda low, high: packed_ref[low:high, :].astype(F32)


def rows_of_either(choice, first_ref, second_ref):
    return lambda low, high: jnp.where(
        choice, first_ref[low:high, :].astype(F32), second_ref[low:high, :].astype(F32)
    )


def half_products(blocks, first, count, factor):
    left = blocks[first : first + count].reshape(count * N, N)
    return lax.dot_general(left, factor.reshape(2 * N, N), LANES_LAST, preferred_element_type=F32).astype(BF16)


def place_halves(products, k, slot, piece):
    lanes = slice(k % 2 * N, (k % 2 + 1) * N)
    for term in range(2):
        products[k // 2, (2 * slot + term) * N : (2 * slot + term + 1) * N, lanes] = piece[:, term * N : (term + 1) * N]


def clear_halves(products, k, slot):
    lanes = slice(k % 2 * N, (k % 2 + 1) * N)
    products[k // 2, 2 * slot * N : (2 * slot + 2) * N, lanes] = jnp.zeros((2 * N, N), BF16)


def second_product(products, pair, factors):
    left = jnp.concatenate([factor[term] for factor in factors for term in range(2)], axis=1)
    right = products[pair, : 2 * N * len(factors), :]
    return jnp.dot(left, right, preferred_element_type=F32)


def inner_kernel(
    own_ref, other_ref, factors_ref, hamiltonian_ref, sum_ref, forms_ref, partial_ref, charge_ref,
    blocks, products, rows,
):
    core = lax.rem(lax.axis_index("ka"), CORES)
    base = SPAN - (KL - 1) - KL * core
    factors = [factors_ref.at[base + shift] for shift in range(SHIFTS)]
    unpack(rows_of(own_ref), blocks, lambda i: core * KL + i)
    unpack(rows_of(other_ref), blocks, lambda i: (1 - core) * KL + i)
    for k in range(0, KL, 2):
        clear_halves(products, k, 0)
        clear_halves(products, k + 1, CHIP)
    for shift in range(SHIFTS):
        low = max(0, KL - 1 - shift)
        high = min(KL, SHIFTS - shift)
        halves = half_products(blocks, low + shift - (KL - 1), high - low, factors[shift][...])
        for k in range(low, high):
            place_halves(products, k, shift - (KL - 2 - k // 2 * 2), halves[(k - low) * N : (k - low + 1) * N, :])
    for pair in range(KL // 2):
        first = KL - 2 - 2 * pair
        result = second_product(products, pair, factors[first : first + CHIP + 1])
        for member in range(2):
            k = 2 * pair + member
            partial_ref[k] = hamiltonian_ref[k] - result[:, member * N : (member + 1) * N]
    for j in range(forms_ref.shape[0]):
        rows[j : j + 1, :] = jnp.sum(sum_ref[...] * forms_ref[j].astype(F32), axis=0, keepdims=True)
    charge_ref[...] = lane_sums(rows[...])


def turn_kernel(forms_ref, turned_ref, traces_ref, rows):
    row, col = square_iota()
    for j in range(forms_ref.shape[0]):
        rows[j : j + 1, :] = jnp.sum(jnp.where(row == col, forms_ref[j].astype(F32), 0.0), axis=0, keepdims=True)
    traces_ref[...] = lane_sums(rows[...])
    group = N // turned_ref.shape[0]
    for at in range(0, turned_ref.shape[0], 2):
        rows = forms_ref[:, at * group : (at + 2) * group, :].astype(F32)
        for half in range(2):
            part = rows[:, half * group : (half + 1) * group, :]
            turned_ref[at + half] = part.reshape(-1, N).T.astype(BF16)


def side_kernel(second, block_ref, factors_ref, partial_ref, next_ref, blocks, products):
    core = lax.rem(lax.axis_index("ka"), CORES)
    far = own_sum_is_even() != second
    flipped = (core == 1) == far
    last = 2 * SPAN
    unpack(rows_of(block_ref), blocks, lambda i: jnp.where(flipped, KL - 1 - i, i))
    factors = [factors_ref.at[jnp.where(flipped, distance, last - distance)] for distance in range(KL)]
    for k in range(0, KL, 2):
        clear_halves(products, k, k + 1)
    for distance in range(KL):
        halves = half_products(blocks, 0, KL - distance, factors[distance][...])
        for k in range(distance, KL):
            place_halves(products, k, distance, halves[(k - distance) * N : (k - distance + 1) * N, :])
    for pair in range(KL // 2):
        result = second_product(products, pair, factors[: 2 * pair + 2])
        for member in range(2):
            k = 2 * pair + member
            k = jnp.where(flipped, KL - 1 - k, k)
            next_ref[k] = partial_ref[k] - result[:, member * N : (member + 1) * N]


def last_kernel(
    even_ref, odd_ref, factors_ref, partial_ref, turned_ref, traces_ref, charge_ref, level_ref, stats_ref,
    blocks, products, diagonals, squares,
):
    flipped = lax.rem(lax.axis_index("ka"), CORES) == 1
    last = 2 * SPAN
    unpack(rows_of_either(own_sum_is_even(), odd_ref, even_ref), blocks, lambda i: jnp.where(flipped, KL - 1 - i, i))
    factors = [factors_ref.at[jnp.where(flipped, last - distance, distance)] for distance in range(CHIP)]
    for k in range(0, KL, 2):
        clear_halves(products, k, 0)
        clear_halves(products, k + 1, KL)
    for distance in range(1, CHIP):
        low = max(0, KL - distance)
        high = min(KL, CHIP - distance)
        halves = half_products(blocks, distance + low - KL, high - low, factors[distance][...])
        for k in range(low, high):
            place_halves(products, k, distance - (KL - 1 - k // 2 * 2), halves[(k - low) * N : (k - low + 1) * N, :])
    row, col = square_iota()
    for pair in range(KL // 2):
        first = KL - 1 - 2 * pair
        result = second_product(products, pair, factors[first : first + KL + 1])
        for member in range(2):
            k = 2 * pair + member
            k = jnp.where(flipped, KL - 1 - k, k)
            combined = partial_ref[k] - result[:, member * N : (member + 1) * N]
            level = 0.5 * (combined + combined.T)
            level_ref[pl.ds(pl.multiple_of(k * N, N), N), :] = level
            diagonals[pl.ds(k, 1), :] = jnp.sum(jnp.where(row == col, level, 0.0), axis=0, keepdims=True)
            outside = jnp.where(row == col, 0.0, level)
            squares[pl.ds(k, 1), :] = jnp.sum(outside * outside, axis=0, keepdims=True)

    mean = jnp.sum(diagonals[...], axis=1, keepdims=True) / N
    rest = diagonals[...] - mean
    norm = jnp.sum(squares[...] + rest * rest, axis=1, keepdims=True)
    lane = lax.broadcasted_iota(jnp.int32, (KL, N), 1)
    place = lax.broadcasted_iota(jnp.int32, (KL, N), 0)
    group = N // turned_ref.shape[0]
    form_count = turned_ref.shape[2] // group
    table = jnp.zeros((2 * KL * group, group * form_count), F32)
    for at in range(0, N // group, 2):
        lefts = []
        for first in (at * group, (at + 1) * group):
            highs, lows = [], []
            for k in range(KL):
                values = level_ref[k * N + first : k * N + first + group, :]
                highs.append(values.astype(BF16).astype(F32))
                lows.append(values - highs[-1])
            lefts.append(jnp.concatenate(highs + lows, axis=0).astype(BF16))
        table = table + jnp.dot(
            jnp.concatenate(lefts, axis=1), turned_ref[at : at + 2].reshape(2 * N, -1), preferred_element_type=F32
        )
    at_row = lax.broadcasted_iota(jnp.int32, table.shape, 0) % group
    at_lane = lax.broadcasted_iota(jnp.int32, table.shape, 1) % group
    table = jnp.where(at_row == at_lane, table, 0.0)
    table = jnp.sum(table.reshape(2 * KL, group, group * form_count), axis=1)
    table = table[:KL, :] + table[KL:, :]
    high = table.astype(BF16)
    low = (table - high.astype(F32)).astype(BF16)
    of_form = lax.broadcasted_iota(jnp.int32, (2 * group * form_count, form_count), 0) // group % form_count
    ones = lax.broadcasted_iota(jnp.int32, of_form.shape, 1) == of_form
    overlaps = jnp.dot(
        jnp.concatenate([high, low], axis=1), jnp.where(ones, 1.0, 0.0).astype(BF16), preferred_element_type=F32
    )
    overlaps = overlaps - mean * traces_ref[0:1, :]
    numbers = jnp.where(lane == form_count + place, norm, 0.0)
    numbers = numbers + jnp.where(lane == form_count + KL + place, mean, 0.0)
    charge = jnp.concatenate([charge_ref[0:1, :], jnp.zeros((1, N - form_count), F32)], axis=1)
    numbers = jnp.sum(numbers, axis=0, keepdims=True) + charge
    stats = jnp.concatenate([overlaps[k : k + 1, :] for k in range(KL)] + [numbers], axis=1)
    stats_ref[...] = jnp.broadcast_to(stats, stats_ref.shape)


def final_kernel(
    stats_ref, level_ref, forms_ref, coupling_ref, occupations_ref, fock_hbm, density_hbm, fock, density, sent
):
    form_count = forms_ref.shape[0]
    count = stats_ref.shape[0]
    total = count * KL
    overlap_count = KL * form_count
    charge = jnp.sum(stats_ref[:, overlap_count : overlap_count + form_count], axis=0, keepdims=True) / total
    weights = coupling_ref[...] * charge
    row, col = square_iota()
    hartree = jnp.zeros((N, N), F32)
    for j in range(form_count):
        hartree = hartree + weights[:, j : j + 1] * forms_ref[j].astype(F32)
    hartree = 0.5 * (hartree + hartree.T)
    diagonal = jnp.sum(jnp.where(row == col, hartree, 0.0), axis=0, keepdims=True)
    offset = jnp.sum(diagonal, axis=1, keepdims=True) / N
    beside = jnp.where(row == col, 0.0, hartree)
    own = jnp.sum(beside * beside, axis=0, keepdims=True) + (diagonal - offset) ** 2
    own = jnp.sum(own, axis=1, keepdims=True)
    norms_at = overlap_count + form_count
    means = stats_ref[:, norms_at + KL : norms_at + 2 * KL]
    mean = jnp.sum(means, keepdims=True) / total
    cross = [
        jnp.sum(stats_ref[:, k * form_count : (k + 1) * form_count] * weights, axis=1, keepdims=True)
        for k in range(KL)
    ]
    cross = jnp.concatenate(cross, axis=1)
    norms = stats_ref[:, norms_at : norms_at + KL] + 2.0 * cross + own + N * (means - mean) ** 2
    radius = jnp.sqrt(1e-06 + jnp.max(norms, keepdims=True))
    scale = 0.5 / radius
    shift = offset + mean
    eye = jnp.where(row == col, 1.0, 0.0).astype(F32)
    current = []
    for k in range(KL):
        fock[k] = level_ref[k * N : (k + 1) * N, :] + hartree
        filling = occupations_ref[k].astype(F32) / N - 0.5
        current.append((filling + scale * shift) * eye - scale * fock[k])
    copies = [pltpu.make_async_copy(fock, fock_hbm, sent.at[0])]
    copies[0].start()
    for _ in range(NPUR):
        for k in range(KL):
            short = current[k].astype(BF16)
            square = jnp.dot(short, short, preferred_element_type=F32).astype(BF16)
            cube = jnp.dot(square, short, preferred_element_type=F32)
            current[k] = 1.5 * current[k] - 2.0 * cube
    for k in range(KL):
        density[k] = current[k] + 0.5 * eye
        if k % 2 == 1:
            ready = pl.ds(k - 1, 2)
            copies.append(pltpu.make_async_copy(density.at[ready], density_hbm.at[ready], sent.at[(k + 1) // 2]))
            copies[-1].start()
    for copy in copies:
        copy.wait()


def per_device(density, hamiltonian, occupations, form_factors, hartree_forms, coupling):
    kpoint_count = density.shape[0]
    count = lax.axis_size("ka")
    form_count = hartree_forms.shape[0]
    assert kpoint_count == KL and CHIP == SPAN and count % CORES == 0
    shape = jax.ShapeDtypeStruct
    packed, deviation_sum = pl.pallas_call(
        pack_kernel,
        out_shape=(shape((PACK, N), BF16), shape((N, N), F32)),
        in_specs=[HBM],
        out_specs=(VMEM, VMEM),
        scratch_shapes=[pltpu.VMEM((KL, N, N), F32), pltpu.SemaphoreType.DMA(())],
        compiler_params=params(16),
        cost_estimate=pl.CostEstimate(flops=5 * 10**9, bytes_accessed=2 * 10**6, transcendentals=0),
    )(in_hbm(density))
    across = [(d, d ^ 1) for d in range(count)]
    within = [(d, d ^ CORES) for d in range(count)]
    between = [(d, ((d + CORES) ^ CORES) - CORES) for d in range(count)]
    between = [(d, target % count) for d, target in between]
    other = lax.ppermute(packed, "ka", across)
    even = lax.ppermute(packed, "ka", within)
    again = pl.pallas_call(
        copy_kernel, out_shape=shape((PACK, N), BF16), in_specs=[VMEM], out_specs=VMEM, compiler_params=params(16)
    )(packed)
    odd = lax.ppermute(again, "ka", between)
    partial, charge = pl.pallas_call(
        inner_kernel,
        out_shape=(shape((KL, N, N), F32), shape((8, form_count), F32)),
        in_specs=[VMEM] * 6,
        out_specs=(VMEM, VMEM),
        scratch_shapes=[
            pltpu.VMEM((CHIP, N, N), BF16),
            pltpu.VMEM((KL // 2, (CHIP + 1) * 2 * N, 2 * N), BF16),
            pltpu.VMEM((form_count, N), F32),
        ],
        compiler_params=params(28),
        cost_estimate=pl.CostEstimate(flops=5 * 10**9, bytes_accessed=5 * 10**6, transcendentals=0),
    )(packed, other, form_factors, hamiltonian, deviation_sum, hartree_forms)

    side_cost = pl.CostEstimate(flops=2 * 10**9, bytes_accessed=5 * 10**6, transcendentals=0)

    def side(second, block, partial):
        return pl.pallas_call(
            functools.partial(side_kernel, second),
            out_shape=shape((KL, N, N), F32),
            in_specs=[VMEM] * 3,
            out_specs=VMEM,
            scratch_shapes=[pltpu.VMEM((KL, N, N), BF16), pltpu.VMEM((KL // 2, KL * 2 * N, 2 * N), BF16)],
            compiler_params=params(24),
            cost_estimate=side_cost,
        )(block, form_factors, partial)

    partial, hartree_forms = lax.optimization_barrier((partial, hartree_forms))
    turned, traces = pl.pallas_call(
        turn_kernel,
        out_shape=(shape((N * form_count // (2 * N), N, 2 * N), BF16), shape((8, form_count), F32)),
        in_specs=[VMEM],
        out_specs=(VMEM, VMEM),
        scratch_shapes=[pltpu.VMEM((form_count, N), F32)],
        compiler_params=params(16),
        cost_estimate=side_cost,
    )(hartree_forms)
    partial, turned, even = lax.optimization_barrier((partial, turned, even))
    even_across = lax.ppermute(even, "ka", across)
    partial = side(False, even, partial)
    partial, odd = lax.optimization_barrier((partial, odd))
    odd_across = lax.ppermute(odd, "ka", across)
    partial = side(True, odd, partial)
    level, stats = pl.pallas_call(
        last_kernel,
        out_shape=(shape((KL * N, N), F32), shape((count, KL * form_count + N), F32)),
        in_specs=[VMEM] * 7,
        out_specs=(VMEM, VMEM),
        scratch_shapes=[
            pltpu.VMEM((KL, N, N), BF16),
            pltpu.VMEM((KL // 2, (KL + 1) * 2 * N, 2 * N), BF16),
            pltpu.VMEM((KL, N), F32),
            pltpu.VMEM((KL, N), F32),
        ],
        compiler_params=params(28),
    )(even_across, odd_across, form_factors, partial, turned, traces, charge)
    shared = lax.all_to_all(stats, "ka", 0, 0, tiled=True)
    return pl.pallas_call(
        final_kernel,
        out_shape=(shape((KL, N, N), F32), shape((KL, N, N), F32)),
        in_specs=[VMEM] * 4 + [SMEM],
        out_specs=(HBM, HBM),
        scratch_shapes=[pltpu.VMEM((KL, N, N), F32), pltpu.VMEM((KL, N, N), F32), pltpu.SemaphoreType.DMA((1 + KL // 2,))],
        compiler_params=params(24),
    )(shared, level, hartree_forms, coupling.reshape(1, form_count), occupations)


def solution(mesh):
    placed = (P("ka", None, None), P("ka", None, None), P("ka"), P(), P(), P())
    return jax.shard_map(
        per_device,
        mesh=mesh,
        in_specs=placed,
        out_specs=(P("ka", None, None), P("ka", None, None)),
        check_vma=False,
    )
```

```python
import functools

import jax
import jax.numpy as jnp
from jax import lax
from jax.experimental import pallas as pl
from jax.experimental.pallas import tpu as pltpu
from jax.sharding import PartitionSpec as P

SPAN = 16
NPUR = 6
N = 128
KL = 8
CORES = 2
CHIP = CORES * KL
PACK = KL // 2 * N + 16
SHIFTS = CHIP + KL - 1
F32 = jnp.float32
BF16 = jnp.bfloat16
VMEM = pl.BlockSpec(memory_space=pltpu.VMEM)
SMEM = pl.BlockSpec(memory_space=pltpu.SMEM)
HBM = pl.BlockSpec(memory_space=pltpu.HBM)
LANES_LAST = (((1,), (1,)), ((), ()))


def square_iota():
    row = lax.broadcasted_iota(jnp.int32, (N, N), 0)
    col = lax.broadcasted_iota(jnp.int32, (N, N), 1)
    return row, col


def in_hbm(array):
    return pltpu.with_memory_space_constraint(array, pltpu.HBM)


def params(mib):
    return pltpu.CompilerParams(vmem_limit_bytes=mib << 20)


def lane_sums(rows):
    return lax.dot_general(
        jnp.ones((8, N), F32), rows, LANES_LAST, precision=lax.Precision.HIGHEST, preferred_element_type=F32
    )


def pack_kernel(density_hbm, packed_ref, sum_ref, density, arrived):
    copy = pltpu.make_async_copy(density_hbm, density, arrived)
    copy.start()
    row, col = square_iota()
    half_eye = jnp.where(row == col, 0.5, 0.0).astype(F32)
    total = jnp.zeros((N, N), F32)
    diagonals = []
    copy.wait()
    for pair in range(KL // 2):
        parts = []
        for member in range(2):
            deviation = (density[2 * pair + member] - half_eye).astype(BF16).astype(F32)
            total = total + deviation
            parts.append(0.5 * (deviation + deviation.T))
        packed_ref[pair * N : (pair + 1) * N, :] = jnp.where(row <= col, parts[0], parts[1]).astype(BF16)
        diagonals.append(jnp.sum(jnp.where(row == col, parts[1], 0.0), axis=0, keepdims=True))
    diagonals.append(jnp.zeros((16 - KL // 2, N), F32))
    packed_ref[KL // 2 * N :, :] = jnp.concatenate(diagonals, axis=0).astype(BF16)
    sum_ref[...] = total


def copy_kernel(packed_ref, again_ref):
    again_ref[...] = packed_ref[...]


def unpack(load, blocks, place):
    row, col = square_iota()
    diagonals = load(KL // 2 * N, PACK)
    for pair in range(KL // 2):
        both = load(pair * N, (pair + 1) * N)
        flipped = both.T
        blocks[place(2 * pair)] = jnp.where(row <= col, both, flipped).astype(BF16)
        second = jnp.where(row > col, both, jnp.where(row < col, flipped, diagonals[pair : pair + 1, :]))
        blocks[place(2 * pair + 1)] = second.astype(BF16)


def own_sum_is_even():
    index = lax.axis_index("ka")
    return lax.rem(index // CORES + index, 2) == 0


def rows_of(packed_ref):
    return lambda low, high: packed_ref[low:high, :].astype(F32)


def rows_of_either(choice, first_ref, second_ref):
    return lambda low, high: jnp.where(
        choice, first_ref[low:high, :].astype(F32), second_ref[low:high, :].astype(F32)
    )


def half_products(blocks, first, count, factor):
    left = blocks[first : first + count].reshape(count * N, N)
    return lax.dot_general(left, factor.reshape(2 * N, N), LANES_LAST, preferred_element_type=F32).astype(BF16)


def place_halves(products, k, slot, piece):
    lanes = slice(k % 2 * N, (k % 2 + 1) * N)
    for term in range(2):
        products[k // 2, (2 * slot + term) * N : (2 * slot + term + 1) * N, lanes] = piece[:, term * N : (term + 1) * N]


def clear_halves(products, k, slot):
    lanes = slice(k % 2 * N, (k % 2 + 1) * N)
    products[k // 2, 2 * slot * N : (2 * slot + 2) * N, lanes] = jnp.zeros((2 * N, N), BF16)


def second_product(products, pair, factors):
    left = jnp.concatenate([factor[term] for factor in factors for term in range(2)], axis=1)
    right = products[pair, : 2 * N * len(factors), :]
    return jnp.dot(left, right, preferred_element_type=F32)


def inner_kernel(
    own_ref, other_ref, factors_ref, hamiltonian_ref, sum_ref, forms_ref, partial_ref, charge_ref,
    blocks, products, rows,
):
    core = lax.rem(lax.axis_index("ka"), CORES)
    base = SPAN - (KL - 1) - KL * core
    factors = [factors_ref.at[base + shift] for shift in range(SHIFTS)]
    unpack(rows_of(own_ref), blocks, lambda i: core * KL + i)
    unpack(rows_of(other_ref), blocks, lambda i: (1 - core) * KL + i)
    for k in range(0, KL, 2):
        clear_halves(products, k, 0)
        clear_halves(products, k + 1, CHIP)
    for shift in range(SHIFTS):
        low = max(0, KL - 1 - shift)
        high = min(KL, SHIFTS - shift)
        halves = half_products(blocks, low + shift - (KL - 1), high - low, factors[shift][...])
        for k in range(low, high):
            place_halves(products, k, shift - (KL - 2 - k // 2 * 2), halves[(k - low) * N : (k - low + 1) * N, :])
    for pair in range(KL // 2):
        first = KL - 2 - 2 * pair
        result = second_product(products, pair, factors[first : first + CHIP + 1])
        for member in range(2):
            k = 2 * pair + member
            partial_ref[k] = hamiltonian_ref[k] - result[:, member * N : (member + 1) * N]
    for j in range(forms_ref.shape[0]):
        rows[j : j + 1, :] = jnp.sum(sum_ref[...] * forms_ref[j].astype(F32), axis=0, keepdims=True)
    charge_ref[...] = lane_sums(rows[...])


def turn_kernel(forms_ref, turned_ref, traces_ref, rows):
    row, col = square_iota()
    for j in range(forms_ref.shape[0]):
        rows[j : j + 1, :] = jnp.sum(jnp.where(row == col, forms_ref[j].astype(F32), 0.0), axis=0, keepdims=True)
    traces_ref[...] = lane_sums(rows[...])
    group = N // turned_ref.shape[0]
    for at in range(0, turned_ref.shape[0], 2):
        rows = forms_ref[:, at * group : (at + 2) * group, :].astype(F32)
        for half in range(2):
            part = rows[:, half * group : (half + 1) * group, :]
            turned_ref[at + half] = part.reshape(-1, N).T.astype(BF16)


def side_kernel(second, block_ref, factors_ref, partial_ref, next_ref, blocks, products):
    core = lax.rem(lax.axis_index("ka"), CORES)
    far = own_sum_is_even() != second
    flipped = (core == 1) == far
    last = 2 * SPAN
    unpack(rows_of(block_ref), blocks, lambda i: jnp.where(flipped, KL - 1 - i, i))
    factors = [factors_ref.at[jnp.where(flipped, distance, last - distance)] for distance in range(KL)]
    for k in range(0, KL, 2):
        clear_halves(products, k, k + 1)
    for distance in range(KL):
        halves = half_products(blocks, 0, KL - distance, factors[distance][...])
        for k in range(distance, KL):
            place_halves(products, k, distance, halves[(k - distance) * N : (k - distance + 1) * N, :])
    for pair in range(KL // 2):
        result = second_product(products, pair, factors[: 2 * pair + 2])
        for member in range(2):
            k = 2 * pair + member
            k = jnp.where(flipped, KL - 1 - k, k)
            next_ref[k] = partial_ref[k] - result[:, member * N : (member + 1) * N]


def last_kernel(
    even_ref, odd_ref, factors_ref, partial_ref, turned_ref, traces_ref, charge_ref, level_ref, stats_ref,
    blocks, products, diagonals, squares,
):
    flipped = lax.rem(lax.axis_index("ka"), CORES) == 1
    last = 2 * SPAN
    unpack(rows_of_either(own_sum_is_even(), odd_ref, even_ref), blocks, lambda i: jnp.where(flipped, KL - 1 - i, i))
    factors = [factors_ref.at[jnp.where(flipped, last - distance, distance)] for distance in range(CHIP)]
    for k in range(0, KL, 2):
        clear_halves(products, k, 0)
        clear_halves(products, k + 1, KL)
    for distance in range(1, CHIP):
        low = max(0, KL - distance)
        high = min(KL, CHIP - distance)
        halves = half_products(blocks, distance + low - KL, high - low, factors[distance][...])
        for k in range(low, high):
            place_halves(products, k, distance - (KL - 1 - k // 2 * 2), halves[(k - low) * N : (k - low + 1) * N, :])
    row, col = square_iota()
    for pair in range(KL // 2):
        first = KL - 1 - 2 * pair
        result = second_product(products, pair, factors[first : first + KL + 1])
        for member in range(2):
            k = 2 * pair + member
            k = jnp.where(flipped, KL - 1 - k, k)
            combined = partial_ref[k] - result[:, member * N : (member + 1) * N]
            level = 0.5 * (combined + combined.T)
            level_ref[pl.ds(pl.multiple_of(k * N, N), N), :] = level
            diagonals[pl.ds(k, 1), :] = jnp.sum(jnp.where(row == col, level, 0.0), axis=0, keepdims=True)
            outside = jnp.where(row == col, 0.0, level)
            squares[pl.ds(k, 1), :] = jnp.sum(outside * outside, axis=0, keepdims=True)

    mean = jnp.sum(diagonals[...], axis=1, keepdims=True) / N
    rest = diagonals[...] - mean
    norm = jnp.sum(squares[...] + rest * rest, axis=1, keepdims=True)
    lane = lax.broadcasted_iota(jnp.int32, (KL, N), 1)
    place = lax.broadcasted_iota(jnp.int32, (KL, N), 0)
    group = N // turned_ref.shape[0]
    form_count = turned_ref.shape[2] // group
    table = jnp.zeros((2 * KL * group, group * form_count), F32)
    for at in range(0, N // group, 2):
        lefts = []
        for first in (at * group, (at + 1) * group):
            highs, lows = [], []
            for k in range(KL):
                values = level_ref[k * N + first : k * N + first + group, :]
                highs.append(values.astype(BF16).astype(F32))
                lows.append(values - highs[-1])
            lefts.append(jnp.concatenate(highs + lows, axis=0).astype(BF16))
        table = table + jnp.dot(
            jnp.concatenate(lefts, axis=1), turned_ref[at : at + 2].reshape(2 * N, -1), preferred_element_type=F32
        )
    at_row = lax.broadcasted_iota(jnp.int32, table.shape, 0) % group
    at_lane = lax.broadcasted_iota(jnp.int32, table.shape, 1) % group
    table = jnp.where(at_row == at_lane, table, 0.0)
    table = jnp.sum(table.reshape(2 * KL, group, group * form_count), axis=1)
    table = table[:KL, :] + table[KL:, :]
    high = table.astype(BF16)
    low = (table - high.astype(F32)).astype(BF16)
    of_form = lax.broadcasted_iota(jnp.int32, (2 * group * form_count, form_count), 0) // group % form_count
    ones = lax.broadcasted_iota(jnp.int32, of_form.shape, 1) == of_form
    overlaps = jnp.dot(
        jnp.concatenate([high, low], axis=1), jnp.where(ones, 1.0, 0.0).astype(BF16), preferred_element_type=F32
    )
    overlaps = overlaps - mean * traces_ref[0:1, :]
    numbers = jnp.where(lane == form_count + place, norm, 0.0)
    numbers = numbers + jnp.where(lane == form_count + KL + place, mean, 0.0)
    charge = jnp.concatenate([charge_ref[0:1, :], jnp.zeros((1, N - form_count), F32)], axis=1)
    numbers = jnp.sum(numbers, axis=0, keepdims=True) + charge
    stats = jnp.concatenate([overlaps[k : k + 1, :] for k in range(KL)] + [numbers], axis=1)
    stats_ref[...] = jnp.broadcast_to(stats[None], stats_ref.shape)


def final_kernel(
    stats_ref, level_ref, forms_ref, coupling_ref, occupations_ref, fock_hbm, density_hbm, fock, density, sent
):
    form_count = forms_ref.shape[0]
    count = stats_ref.shape[0]
    total = count * KL
    overlap_count = KL * form_count
    charge = jnp.sum(stats_ref[:, overlap_count : overlap_count + form_count], axis=0, keepdims=True) / total
    weights = coupling_ref[...] * charge
    row, col = square_iota()
    hartree = jnp.zeros((N, N), F32)
    for j in range(form_count):
        hartree = hartree + weights[:, j : j + 1] * forms_ref[j].astype(F32)
    hartree = 0.5 * (hartree + hartree.T)
    diagonal = jnp.sum(jnp.where(row == col, hartree, 0.0), axis=0, keepdims=True)
    offset = jnp.sum(diagonal, axis=1, keepdims=True) / N
    beside = jnp.where(row == col, 0.0, hartree)
    own = jnp.sum(beside * beside, axis=0, keepdims=True) + (diagonal - offset) ** 2
    own = jnp.sum(own, axis=1, keepdims=True)
    norms_at = overlap_count + form_count
    means = stats_ref[:, norms_at + KL : norms_at + 2 * KL]
    mean = jnp.sum(means, keepdims=True) / total
    cross = [
        jnp.sum(stats_ref[:, k * form_count : (k + 1) * form_count] * weights, axis=1, keepdims=True)
        for k in range(KL)
    ]
    cross = jnp.concatenate(cross, axis=1)
    norms = stats_ref[:, norms_at : norms_at + KL] + 2.0 * cross + own + N * (means - mean) ** 2
    radius = jnp.sqrt(1e-06 + jnp.max(norms, keepdims=True))
    scale = 0.5 / radius
    shift = offset + mean
    eye = jnp.where(row == col, 1.0, 0.0).astype(F32)
    current = []
    for k in range(KL):
        fock[k] = level_ref[k * N : (k + 1) * N, :] + hartree
        filling = occupations_ref[k].astype(F32) / N - 0.5
        current.append((filling + scale * shift) * eye - scale * fock[k])
    copies = [pltpu.make_async_copy(fock, fock_hbm, sent.at[0])]
    copies[0].start()
    for _ in range(NPUR):
        for k in range(KL):
            short = current[k].astype(BF16)
            square = jnp.dot(short, short, preferred_element_type=F32).astype(BF16)
            cube = jnp.dot(square, short, preferred_element_type=F32)
            current[k] = 1.5 * current[k] - 2.0 * cube
    for k in range(KL):
        density[k] = current[k] + 0.5 * eye
        if k % 2 == 1:
            ready = pl.ds(k - 1, 2)
            copies.append(pltpu.make_async_copy(density.at[ready], density_hbm.at[ready], sent.at[(k + 1) // 2]))
            copies[-1].start()
    for copy in copies:
        copy.wait()


def per_device(density, hamiltonian, occupations, form_factors, hartree_forms, coupling):
    kpoint_count = density.shape[0]
    count = lax.axis_size("ka")
    form_count = hartree_forms.shape[0]
    assert kpoint_count == KL and CHIP == SPAN and count % CORES == 0
    shape = jax.ShapeDtypeStruct
    packed, deviation_sum = pl.pallas_call(
        pack_kernel,
        out_shape=(shape((PACK, N), BF16), shape((N, N), F32)),
        in_specs=[HBM],
        out_specs=(VMEM, VMEM),
        scratch_shapes=[pltpu.VMEM((KL, N, N), F32), pltpu.SemaphoreType.DMA(())],
        compiler_params=params(16),
        cost_estimate=pl.CostEstimate(flops=5 * 10**9, bytes_accessed=2 * 10**6, transcendentals=0),
    )(in_hbm(density))
    across = [(d, d ^ 1) for d in range(count)]
    within = [(d, d ^ CORES) for d in range(count)]
    between = [(d, ((d + CORES) ^ CORES) - CORES) for d in range(count)]
    between = [(d, target % count) for d, target in between]
    other = lax.ppermute(packed, "ka", across)
    even = lax.ppermute(packed, "ka", within)
    again = pl.pallas_call(
        copy_kernel, out_shape=shape((PACK, N), BF16), in_specs=[VMEM], out_specs=VMEM, compiler_params=params(16)
    )(packed)
    odd = lax.ppermute(again, "ka", between)
    partial, charge = pl.pallas_call(
        inner_kernel,
        out_shape=(shape((KL, N, N), F32), shape((8, form_count), F32)),
        in_specs=[VMEM] * 6,
        out_specs=(VMEM, VMEM),
        scratch_shapes=[
            pltpu.VMEM((CHIP, N, N), BF16),
            pltpu.VMEM((KL // 2, (CHIP + 1) * 2 * N, 2 * N), BF16),
            pltpu.VMEM((form_count, N), F32),
        ],
        compiler_params=params(28),
        cost_estimate=pl.CostEstimate(flops=5 * 10**9, bytes_accessed=5 * 10**6, transcendentals=0),
    )(packed, other, form_factors, hamiltonian, deviation_sum, hartree_forms)

    side_cost = pl.CostEstimate(flops=2 * 10**9, bytes_accessed=5 * 10**6, transcendentals=0)

    def side(second, block, partial):
        return pl.pallas_call(
            functools.partial(side_kernel, second),
            out_shape=shape((KL, N, N), F32),
            in_specs=[VMEM] * 3,
            out_specs=VMEM,
            scratch_shapes=[pltpu.VMEM((KL, N, N), BF16), pltpu.VMEM((KL // 2, KL * 2 * N, 2 * N), BF16)],
            compiler_params=params(24),
            cost_estimate=side_cost,
        )(block, form_factors, partial)

    partial, hartree_forms = lax.optimization_barrier((partial, hartree_forms))
    turned, traces = pl.pallas_call(
        turn_kernel,
        out_shape=(shape((N * form_count // (2 * N), N, 2 * N), BF16), shape((8, form_count), F32)),
        in_specs=[VMEM],
        out_specs=(VMEM, VMEM),
        scratch_shapes=[pltpu.VMEM((form_count, N), F32)],
        compiler_params=params(16),
        cost_estimate=side_cost,
    )(hartree_forms)
    partial, turned, even = lax.optimization_barrier((partial, turned, even))
    even_across = lax.ppermute(even, "ka", across)
    partial = side(False, even, partial)
    partial, odd = lax.optimization_barrier((partial, odd))
    odd_across = lax.ppermute(odd, "ka", across)
    partial = side(True, odd, partial)
    level, stats = pl.pallas_call(
        last_kernel,
        out_shape=(shape((KL * N, N), F32), shape((count, 1, KL * form_count + N), F32)),
        in_specs=[VMEM] * 7,
        out_specs=(VMEM, VMEM),
        scratch_shapes=[
            pltpu.VMEM((KL, N, N), BF16),
            pltpu.VMEM((KL // 2, (KL + 1) * 2 * N, 2 * N), BF16),
            pltpu.VMEM((KL, N), F32),
            pltpu.VMEM((KL, N), F32),
        ],
        compiler_params=params(28),
    )(even_across, odd_across, form_factors, partial, turned, traces, charge)
    shared = lax.all_to_all(stats, "ka", 0, 0, tiled=True).reshape(count, -1)
    return pl.pallas_call(
        final_kernel,
        out_shape=(shape((KL, N, N), F32), shape((KL, N, N), F32)),
        in_specs=[VMEM] * 4 + [SMEM],
        out_specs=(HBM, HBM),
        scratch_shapes=[pltpu.VMEM((KL, N, N), F32), pltpu.VMEM((KL, N, N), F32), pltpu.SemaphoreType.DMA((1 + KL // 2,))],
        compiler_params=params(24),
    )(shared, level, hartree_forms, coupling.reshape(1, form_count), occupations)


def solution(mesh):
    placed = (P("ka", None, None), P("ka", None, None), P("ka"), P(), P(), P())
    return jax.shard_map(
        per_device,
        mesh=mesh,
        in_specs=placed,
        out_specs=(P("ka", None, None), P("ka", None, None)),
        check_vma=False,
    )
```
